256 devices in a mesh: dp: 32 (over z_lo, x, core), fsdp: 8 (over y, z_hi).
Axes of the slice: x: 4, y: 4, z: 8 (z_hi: 2, z_lo: 4; z = z_hi * 4 + z_lo), core: 2. Of those that a mesh axis runs over, the one named last changes fastest.
Arguments:
- latents: bfloat16 [128, 256, 4096], P('dp', 'fsdp'), may hold values from -6 to 6
- w_query: bfloat16 [4096, 2048], P('fsdp'), may hold values from -0.09375 to 0.09375
- w_out: bfloat16 [2048, 4096], P('fsdp'), may hold values from -0.125 to 0.125
- text_cache: bfloat16 [4, 128, 4096], replicated, may hold values from -128 to 128
- branch_counts: int32 [128], replicated, may hold values from 1 to 4, 192 in all
- branch_conds: int32 [128, 4], replicated, may hold values from 0 to 3
- guide_weights: int32 [4], replicated, may hold values from 1 to 8
- mod_scale: float32 [128, 4096], P('dp'), may hold values from -3 to 3
- mod_shift: float32 [128, 4096], P('dp'), may hold values from -6 to 6
Outputs:
- mixed: bfloat16 [128, 256, 4096], P('dp', 'fsdp')
The draws below stay inside these ranges and needn't reach their ends.
Inputs may be any that keep to these rules, and one draw needn't show every extreme that they name: `branch_counts`: the counts sum to 192. `branch_conds`: entries past a latent's count are not used.
All inputs are finite; a program needn't handle non-finite values.
Results may differ from the reference program's by a relative error of at most 0.0086.
Values may be sent and summed in bfloat16 or wider, within the bound.
A program may use at most 128 MiB of HBM per device.

```python
import math
import jax
import jax.numpy as jnp
import numpy as np
from jax import lax

D = 4096
HEADS = 16
HDIM = 128
TEXT = 128
NCOND = 4
SLOTS = 4
HQ = 2048
LATENTS = 128
SEQ = 256
BRANCHES = 192


def draw_text_cache(key, part):
    key = jax.random.fold_in(key, 7)
    base_key = jax.random.fold_in(key, 0)
    shape = (NCOND, TEXT, 2 * HEADS * HDIM)
    values = jnp.clip(jax.random.normal(base_key, shape, jnp.float32), -4.0, 4.0)
    return values.astype(jnp.bfloat16)


def set_ends(drawn, own_key, smallest, high):
    index_at = [jax.random.randint(jax.random.fold_in(own_key, axis), (), 0, length) for axis, length in enumerate(drawn.shape)]
    main_axis = drawn.shape.index(max(drawn.shape))
    beside = index_at[:main_axis] + [(index_at[main_axis] + 1) % drawn.shape[main_axis]] + index_at[main_axis + 1:]
    return drawn.at[tuple(index_at)].set(smallest).at[tuple(beside)].set(high)


def level_of(own_key, extent, pieces, least, largest):
    def one(axis_at, blocks):
        steps = jax.random.uniform(jax.random.fold_in(jax.random.fold_in(own_key, 6), axis_at), (blocks,), jnp.float32, least / len(pieces), largest / len(pieces))
        return jnp.repeat(jnp.exp(steps), extent[axis_at] // blocks).reshape((-1,) + (1,) * (len(extent) - axis_at - 1))

    loudness = one(*pieces[0])
    for cut in pieces[1:]:
        loudness = loudness * one(*cut)
    return loudness


def length_profile(count, total, most, lean):
    loads = [(1 << 20) // math.isqrt(grade ** lean) + 1 for grade in range(2, count + 1)]
    rest, counts = total - most - (count - 1), [1] * (count - 1)
    while rest > 0:
        candidates = [i for i in range(count - 1) if counts[i] < most]
        pool, remaining = sum([loads[i] for i in candidates]), rest
        for i in candidates:
            addition = min(most - counts[i], max(1, remaining * loads[i] // pool), rest)
            counts[i] = counts[i] + addition
            rest = rest - addition
    return np.array([most] + counts)


def ragged_sizes(rng, number_of, total, most, skew):
    if number_of == 2:
        one = jax.random.randint(rng, (), max(1, total - most), min(most, total - 1) + 1)
        return jnp.stack([one, total - one])
    tallies = jnp.asarray(length_profile(number_of, total, most, skew), jnp.int32)
    couples = (number_of - 1) // 2
    donor, receiver = tallies[1:1 + 2 * couples:2], tallies[2:2 + 2 * couples:2]
    margin = jnp.minimum(donor - 1, most - receiver)
    passed = jax.random.randint(jax.random.fold_in(rng, 1), (couples,), 0, 1 << 20) % (margin + 1)
    tallies = tallies.at[1:1 + 2 * couples:2].set(donor - passed).at[2:2 + 2 * couples:2].set(receiver + passed)
    return tallies[jax.random.permutation(jax.random.fold_in(rng, 2), number_of)]


def bell_draw(own_key, dims, scale, bound, shards=(), dtype=jnp.bfloat16):
    values = jax.random.normal(own_key, dims, jnp.float32) * scale
    if len(shards) > 0:
        values = level_of(own_key, dims, shards, -0.22, 0.18) * values
    return jnp.clip(values, min=-bound, max=bound).astype(dtype)


def setup_inputs(seed: int = 0) -> dict:
    seeds = jax.random.split(jax.random.key(seed), 10)
    latents = bell_draw(seeds[0], (LATENTS, SEQ, D), 1.0, 6.0, ((0, 32), (1, 8)))
    w_query = bell_draw(seeds[1], (D, HQ), D ** -0.5, 0.09375, ((0, 8),))
    w_out = bell_draw(seeds[2], (HQ, D), HQ ** -0.5, 0.125, ((0, 8),))
    text_cache = draw_text_cache(jax.random.fold_in(seeds[9], 71), 0)
    branch_counts = ragged_sizes(seeds[4], LATENTS, BRANCHES, SLOTS, 2).astype(jnp.int32)
    branch_conds = set_ends(jax.random.randint(seeds[5], (LATENTS, SLOTS), 0, NCOND), jax.random.fold_in(seeds[5], 1), 0, NCOND - 1).astype(jnp.int32)
    guide_weights = set_ends(jax.random.randint(seeds[6], (SLOTS,), 1, 9), jax.random.fold_in(seeds[6], 1), 1, 8).astype(jnp.int32)
    mod_scale = bell_draw(seeds[7], (LATENTS, D), 0.5, 3.0, ((0, 32),), jnp.float32)
    mod_shift = bell_draw(seeds[8], (LATENTS, D), 1.0, 6.0, ((0, 32),), jnp.float32)
    return {"latents": latents, "w_query": w_query, "w_out": w_out, "text_cache": text_cache, "branch_counts": branch_counts, "branch_conds": branch_conds, "guide_weights": guide_weights, "mod_scale": mod_scale, "mod_shift": mod_shift}


def layer_norm(hidden):
    center = lax.optimization_barrier(jnp.mean(hidden, axis=-1, keepdims=True))
    spread = lax.optimization_barrier(jnp.mean((hidden - center) ** 2, axis=-1, keepdims=True))
    return (hidden - center) * lax.rsqrt(spread + 1e-06)

def attend(query_rows, table_row):
    total_rows = query_rows.shape[0]
    query_h = query_rows.reshape(total_rows, HEADS, HDIM).astype(jnp.float32)
    key_part = table_row[:, :HQ].reshape(TEXT, HEADS, HDIM).astype(jnp.float32)
    value_part = table_row[:, HQ:].reshape(TEXT, HEADS, HDIM).astype(jnp.float32)
    scores = jnp.einsum('rhd,thd->hrt', query_h, key_part) * (1.0 / math.sqrt(HDIM))
    peak = lax.optimization_barrier(jnp.max(scores, axis=-1, keepdims=True))
    expd = jnp.exp(scores - peak)
    softmax_w = (expd / lax.optimization_barrier(jnp.sum(expd, axis=-1, keepdims=True))).astype(jnp.bfloat16)
    result = jnp.einsum('hrt,thd->rhd', softmax_w.astype(jnp.float32), value_part)
    return result.reshape(total_rows, HQ).astype(jnp.bfloat16)

def reference(latents, w_query, w_out, text_cache, branch_counts, branch_conds, guide_weights, mod_scale, mod_shift):
    queries = jnp.dot(latents.reshape(-1, D), w_query, preferred_element_type=jnp.float32)
    queries = queries.astype(jnp.bfloat16).reshape(LATENTS, SEQ, HQ)
    guide_float = guide_weights.astype(jnp.float32)

    def one_latent(items):
        latent_x, latent_q, count_here, cond_row, scale_row, shift_row = items

        def per_slot(slot_idx, carry):
            numer, denom = carry
            table_row = lax.dynamic_index_in_dim(text_cache, cond_row[slot_idx], 0, keepdims=False)
            attended = attend(latent_q, table_row)
            hidden = latent_x.astype(jnp.float32) + jnp.dot(attended, w_out, preferred_element_type=jnp.float32)
            weight = guide_float[slot_idx]
            return (numer + weight * layer_norm(hidden), denom + weight)
        start = (jnp.zeros((SEQ, D), jnp.float32), jnp.zeros((), jnp.float32))
        numer, denom = lax.fori_loop(0, count_here, per_slot, start)
        combined = (numer / denom).astype(jnp.bfloat16)
        return (combined.astype(jnp.float32) * (1.0 + scale_row) + shift_row).astype(jnp.bfloat16)
    return lax.map(one_latent, (latents, queries, branch_counts, branch_conds, mod_scale, mod_shift))
```

```python
import functools
import math

import jax
import jax.numpy as jnp
from jax import lax
from jax.experimental import pallas as pl
from jax.experimental.pallas import tpu as pltpu
from jax.sharding import PartitionSpec as P

HDIM = 128
MESH = pl.DeviceIdType.MESH
LAG = 3
KGROUPS = 4
RELAY_LAG = 2
PREFS = {
    "x": (-1.1011020595399832, -1.9026346360323592, 2.1056340006474246),
    "y": (2.9389532323178447, -2.1789154677931455, 2.885831829951437),
    "z": (-2.8608332355771946, 2.8185845334998927, 1.2925265631373692),
}
CHAIN_PREF = 2.5997267012272784
QUERY_PREF = 5.0
GROUP_PREF = 1.0


def moved(link, place, piece):
    dy, h, k, r = piece
    if link == 0:
        return place, (dy, h, k, (r + 1) % 4)
    if link == 1:
        return place, ((dy + 1) % 4, h, k, r)
    if place < 3:
        return place + 1, piece
    return 0, (dy, 1 - h, k, r)


def make_rounds():
    pieces = [
        (dy, h, k, r) for dy in range(4) for h in range(2) for k in range(KGROUPS) for r in range(4)
    ]
    ready = [{p: 0 if p[:2] == (0, 0) else 1 << 30 for p in pieces} for _ in range(4)]
    taken = [{p: p[:2] == (0, 0) for p in pieces} for _ in range(4)]
    worth = {}
    for link, name in enumerate("xyz"):
        half, depth, column = PREFS[name]
        for p in pieces:
            worth[link, p] = (
                (QUERY_PREF if p[2] < KGROUPS // 2 else 0.0)
                - GROUP_PREF * p[2]
                + half * p[1]
                + depth * p[0]
                + column * p[3]
            )
    left = 4 * (len(pieces) - KGROUPS * 4)
    rounds = []
    while left:
        now = len(rounds)
        row = [[None] * 4 for _ in range(3)]
        for link in (2, 1, 0):
            for place in range(4):
                best, best_worth = None, -1e18
                for p in pieces:
                    if ready[place][p] <= now:
                        to, there = moved(link, place, p)
                        if not taken[to][there]:
                            w = worth[link, there]
                            if link == 2:
                                w += CHAIN_PREF * there[1] * (3 - to)
                            if w > best_worth:
                                best, best_worth = (p, to, there), w
                if best is not None:
                    p, to, there = best
                    taken[to][there] = True
                    ready[to][there] = now + LAG
                    left -= 1
                    row[link][place] = p
        rounds.append(row)
    return rounds, ready


def arrivals_of(rounds):
    result = []
    for row in rounds:
        got = [[None] * 4 for _ in range(3)]
        for link in range(3):
            for place in range(4):
                if row[link][place] is not None:
                    to, there = moved(link, place, row[link][place])
                    got[link][to] = there
        result.append(got)
    return result


def shard_ready(ready, groups):
    result = {}
    for dy in range(4):
        for h in range(2):
            last = 0
            if (dy, h) != (0, 0):
                for place in range(4):
                    for k in groups:
                        for r in range(4):
                            mine = ready[place][dy, h, k, r]
                            other = ready[3 - place][(4 - dy) % 4, h, k, r] + RELAY_LAG
                            last = max(last, mine, other)
            result[dy, h] = last
    return result


def kernel(
    n_dp,
    lat_ref,
    wq_ref,
    wo_ref,
    text_ref,
    counts_ref,
    conds_ref,
    guide_ref,
    scale_ref,
    shift_ref,
    out_ref,
    wq,
    wo,
    x_buf,
    text,
    q_acc,
    att,
    acc,
    send_sem,
    recv_sem,
    relay_sem,
    sib_sem,
    local_sem,
):
    rounds, ready = make_rounds()
    arrivals = arrivals_of(rounds)
    n_rounds = len(rounds)
    dp, fs = lax.axis_index("dp"), lax.axis_index("fsdp")
    core, x_at, z_lo = dp % 2, (dp // 2) % 4, dp // 8
    y_at, z_hi = fs // 2, fs % 2
    sign = 1 - 2 * core
    column = (4 + sign * x_at) % 4
    place = z_lo + core * (3 - 2 * z_lo)
    z_next = (z_hi * 4 + z_lo + 8 + sign) % 8
    z_prev = (z_hi * 4 + z_lo + 8 - sign) % 8
    targets = (
        (z_lo * 8 + ((x_at + 4 + sign) % 4) * 2 + core, fs),
        (dp, ((y_at + 4 + sign) % 4) * 2 + z_hi),
        ((z_next % 4) * 8 + x_at * 2 + core, y_at * 2 + z_next // 4),
    )
    sources = (
        (z_lo * 8 + ((x_at + 4 - sign) % 4) * 2 + core, fs),
        (dp, ((y_at + 4 - sign) % 4) * 2 + z_hi),
        ((z_prev % 4) * 8 + x_at * 2 + core, y_at * 2 + z_prev // 4),
    )
    sibling = (dp + sign, fs)

    fetches = [
        pltpu.make_async_copy(wq_ref, wq.at[fs], local_sem.at[0]),
        pltpu.make_async_copy(wo_ref, wo.at[fs], local_sem.at[1]),
        pltpu.make_async_copy(lat_ref, x_buf, local_sem.at[2]),
        pltpu.make_async_copy(text_ref, text, local_sem.at[3]),
    ]
    for fetch in fetches:
        fetch.start()
    barrier = pltpu.get_barrier_semaphore()
    for other in sources + (sibling,):
        pl.semaphore_signal(barrier, inc=1, device_id=other, device_id_type=MESH)
    pl.semaphore_wait(barrier, 4)
    fetches[0].wait()
    fetches[1].wait()

    def shard_of(dy, h):
        return ((y_at + 4 - sign * dy) % 4) * 2 + (z_hi + h) % 2

    def pick(options, field):
        values = {p: options[p][field] for p in options}
        if len(set(values.values())) == 1:
            return next(iter(values.values()))
        result, items = None, list(values.items())
        result = items[-1][1]
        for p, v in items[:-1]:
            result = jnp.where(place == p, v, result)
        return result

    def slot(options, weight):
        shard = shard_of(pick(options, 0), pick(options, 1))
        number = (pick(options, 2) % 2) * 4 + (column + 4 - pick(options, 3)) % 4
        if weight == 0:
            return wq.at[shard, pl.ds(pl.multiple_of(core * 256 + number * 32, 32), 32)], shard
        return wo.at[shard, pl.ds(pl.multiple_of(core * 128 + number * 16, 16), 16)], shard

    def for_places(row, action):
        for weight in range(2):
            options = {
                p: row[p] for p in range(4) if row[p] is not None and row[p][2] // 2 == weight
            }
            if not options:
                continue
            if len(options) == 4:
                action(options, weight)
            else:
                here = functools.reduce(jnp.logical_or, [place == p for p in options])
                pl.when(here)(functools.partial(action, options, weight))

    def link_copy(link, step, options, weight):
        ref, _ = slot(options, weight)
        return pltpu.make_async_remote_copy(
            src_ref=ref,
            dst_ref=ref,
            send_sem=send_sem.at[link * n_rounds + step],
            recv_sem=recv_sem.at[link * n_rounds + step],
            device_id=targets[link],
            device_id_type=MESH,
        )

    def relay_copy(link, step, options, weight):
        ref, shard = slot(options, weight)
        return pltpu.make_async_remote_copy(
            src_ref=ref,
            dst_ref=ref,
            send_sem=relay_sem.at[link * n_rounds + step],
            recv_sem=sib_sem.at[weight * 8 + shard],
            device_id=sibling,
            device_id_type=MESH,
        )

    def wait_sibling(weight, shard):
        if weight == 0:
            ref = wq.at[shard, pl.ds(pl.multiple_of((1 - core) * 256, 256), 256)]
        else:
            ref = wo.at[shard, pl.ds(pl.multiple_of((1 - core) * 128, 128), 128)]
        pltpu.make_async_copy(ref, ref, sib_sem.at[weight * 8 + shard]).wait()

    def query_task(index, dy, h):
        shard = shard_of(dy, h)
        if (dy, h) != (0, 0):
            wait_sibling(0, shard)
        rows = x_buf[:, pl.ds(pl.multiple_of(shard * 512, 512), 512)]

        @pl.loop(0, 4)
        def _(tile):
            at = pl.ds(pl.multiple_of(tile * 512, 512), 512)
            part = jnp.dot(rows, wq[shard, :, at], preferred_element_type=jnp.float32)
            if index == 0:
                q_acc[:, at] = part
            else:
                q_acc[:, at] += part

    def attend_task(first, count):
        @pl.loop(first, first + count)
        def _(head):
            at = pl.ds(pl.multiple_of(head * HDIM, HDIM), HDIM)
            value_at = pl.ds(pl.multiple_of(2048 + head * HDIM, HDIM), HDIM)
            queries = q_acc[:, at].astype(jnp.bfloat16)
            for cond in range(4):
                scores = lax.dot_general(
                    queries,
                    text[cond, :, at],
                    (((1,), (1,)), ((), ())),
                    preferred_element_type=jnp.float32,
                ) * (1.0 / math.sqrt(HDIM))
                expd = jnp.exp(scores - jnp.max(scores, axis=-1, keepdims=True))
                probs = (expd / jnp.sum(expd, axis=-1, keepdims=True)).astype(jnp.bfloat16)
                result = jnp.dot(
                    probs, text[cond, :, value_at], preferred_element_type=jnp.float32
                )
                att[pl.ds(cond * 128, 128), at] = result.astype(jnp.bfloat16)

    def out_task(index, dy, h):
        shard = shard_of(dy, h)
        if (dy, h) != (0, 0):
            wait_sibling(1, shard)
        rows_at = pl.ds(pl.multiple_of(shard * 256, 256), 256)

        @pl.loop(0, 8)
        def _(tile):
            at = pl.ds(pl.multiple_of(tile * 512, 512), 512)
            part = jnp.dot(att[:, rows_at], wo[shard, :, at], preferred_element_type=jnp.float32)
            if index == 0:
                base = x_buf[:, at].astype(jnp.float32)
                acc[:, at] = part + jnp.concatenate([base] * 4, axis=0)
            else:
                acc[:, at] += part

    query_ready = shard_ready(ready, range(KGROUPS // 2))
    out_ready = shard_ready(ready, range(KGROUPS // 2, KGROUPS))
    tasks = []
    for i, s in enumerate(sorted(query_ready, key=lambda s: (query_ready[s], s))):
        tasks.append((query_ready[s], functools.partial(query_task, i, *s)))
    for first in range(0, 16, 2):
        tasks.append((0, functools.partial(attend_task, first, 2)))
    for i, s in enumerate(sorted(out_ready, key=lambda s: (out_ready[s], s))):
        tasks.append((out_ready[s], functools.partial(out_task, i, *s)))

    fetched = False
    for step in range(n_rounds + LAG):
        came = step - LAG
        if came >= 0:
            for link in range(3):
                for_places(
                    arrivals[came][link],
                    lambda options, weight, link=link: link_copy(
                        link, came, options, weight
                    ).wait_recv(),
                )
        if step < n_rounds:
            for link in range(3):
                for_places(
                    rounds[step][link],
                    lambda options, weight, link=link: link_copy(
                        link, step, options, weight
                    ).start(),
                )
        if came >= 0:
            for link in range(3):
                for_places(
                    arrivals[came][link],
                    lambda options, weight, link=link: relay_copy(
                        link, came, options, weight
                    ).start(),
                )
        if step >= 1:
            if not fetched:
                fetches[2].wait()
                fetches[3].wait()
                fetched = True
            if tasks and tasks[0][0] <= step:
                tasks.pop(0)[1]()
    for _, task in tasks:
        task()

    @pl.loop(0, 4)
    def _(member):
        latent = dp * 4 + member
        count = counts_ref[latent]
        total = jnp.int32(0)
        weights = [jnp.int32(0)] * 4
        for s in range(4):
            weight = jnp.where(s < count, guide_ref[s], 0)
            total = total + weight
            cond = conds_ref[s, latent]
            weights = [w + jnp.where(cond == c, weight, 0) for c, w in enumerate(weights)]
        total = total.astype(jnp.float32)
        weights = [w.astype(jnp.float32) for w in weights]
        scale = 1.0 + scale_ref[pl.ds(member, 1), :]
        shift = shift_ref[pl.ds(member, 1), :]

        @pl.loop(0, 2)
        def _(block):
            start = pl.multiple_of(member * 32 + block * 16, 16)
            numer = jnp.zeros((16, 4096), jnp.float32)
            for cond in range(4):
                hidden = acc[pl.ds(pl.multiple_of(cond * 128 + start, 16), 16), :]
                center = jnp.mean(hidden, axis=-1, keepdims=True)
                moved_h = hidden - center
                spread = jnp.mean(moved_h * moved_h, axis=-1, keepdims=True)
                numer += moved_h * (weights[cond] * lax.rsqrt(spread + 1e-06))
            combined = (numer / total).astype(jnp.bfloat16).astype(jnp.float32)
            out_ref[pl.ds(start, 16), :] = (combined * scale + shift).astype(jnp.bfloat16)

    for step in range(n_rounds):
        for link in range(3):
            for_places(
                rounds[step][link],
                lambda options, weight, link=link: link_copy(
                    link, step, options, weight
                ).wait_send(),
            )
            for_places(
                arrivals[step][link],
                lambda options, weight, link=link: relay_copy(
                    link, step, options, weight
                ).wait_send(),
            )


def on_device(
    n_dp,
    latents,
    w_query,
    w_out,
    text_cache,
    branch_counts,
    branch_conds,
    guide_weights,
    mod_scale,
    mod_shift,
):
    members, rows_here, width = latents.shape
    rows = members * rows_here
    n_rounds = len(make_rounds()[0])
    anywhere = pl.BlockSpec(memory_space=pl.ANY)
    in_vmem = pl.BlockSpec(memory_space=pltpu.VMEM)
    in_smem = pl.BlockSpec(memory_space=pltpu.SMEM)
    mixed = pl.pallas_call(
        functools.partial(kernel, n_dp),
        out_shape=jax.ShapeDtypeStruct((rows, width), jnp.bfloat16),
        in_specs=[anywhere] * 4 + [in_smem] * 3 + [in_vmem] * 2,
        out_specs=in_vmem,
        scratch_shapes=[
            pltpu.VMEM((8, 512, 2048), jnp.bfloat16),
            pltpu.VMEM((8, 256, 4096), jnp.bfloat16),
            pltpu.VMEM((rows, width), jnp.bfloat16),
            pltpu.VMEM(text_cache.shape, jnp.bfloat16),
            pltpu.VMEM((rows, 2048), jnp.float32),
            pltpu.VMEM((4 * rows, 2048), jnp.bfloat16),
            pltpu.VMEM((4 * rows, width), jnp.float32),
            pltpu.SemaphoreType.DMA((3 * n_rounds,)),
            pltpu.SemaphoreType.DMA((3 * n_rounds,)),
            pltpu.SemaphoreType.DMA((3 * n_rounds,)),
            pltpu.SemaphoreType.DMA((16,)),
            pltpu.SemaphoreType.DMA((4,)),
        ],
        compiler_params=pltpu.CompilerParams(
            collective_id=0, has_side_effects=True, vmem_limit_bytes=58 * 2**20
        ),
        name="gather_and_attend",
    )(
        latents.reshape(rows, width),
        w_query,
        w_out,
        text_cache,
        branch_counts,
        branch_conds.T,
        guide_weights,
        mod_scale,
        mod_shift,
    )
    return mixed.reshape(members, rows_here, width)


def solution(mesh):
    return jax.shard_map(
        functools.partial(on_device, mesh.shape["dp"]),
        mesh=mesh,
        in_specs=(
            P("dp", "fsdp", None),
            P("fsdp", None),
            P("fsdp", None),
            P(),
            P(),
            P(),
            P(),
            P("dp", None),
            P("dp", None),
        ),
        out_specs=P("dp", "fsdp", None),
        check_vma=False,
    )
```

```python
import functools
import math

import jax
import jax.numpy as jnp
from jax import lax
from jax.experimental import pallas as pl
from jax.experimental.pallas import tpu as pltpu
from jax.sharding import PartitionSpec as P

HDIM = 128
MESH = pl.DeviceIdType.MESH
LAG = 3
KGROUPS = 4
RELAY_LAG = 2
PREFS = {
    "x": (1.5859338734408208, 2.214087352289587, 2.9301547809913906),
    "y": (1.1536104177094657, 1.5604518340377975, 1.8994994812664077),
    "z": (-2.091808917993905, 1.831880295654794, -1.8133725211069505),
}
CHAIN_PREF = 2.3398409033170617
GROUP_PREF = 0.5
LINK_ORDER = (0, 2, 1)
ROUND_US = 1.2
QUERY_US, ATTEND_US, OUT_US = 0.27, 0.72, 0.72
LAST_SHARDS = 3


def moved(link, place, piece):
    dy, h, k, r = piece
    if link == 0:
        return place, (dy, h, k, (r + 1) % 4)
    if link == 1:
        return place, ((dy + 1) % 4, h, k, r)
    if place < 3:
        return place + 1, piece
    return 0, (dy, 1 - h, k, r)


def make_rounds():
    pieces = [
        (dy, h, k, r) for dy in range(4) for h in range(2) for k in range(KGROUPS) for r in range(4)
    ]
    ready = [{p: 0 if p[:2] == (0, 0) else 1 << 30 for p in pieces} for _ in range(4)]
    taken = [{p: p[:2] == (0, 0) for p in pieces} for _ in range(4)]
    worth = {}
    for link, name in enumerate("xyz"):
        half, depth, column = PREFS[name]
        for p in pieces:
            worth[link, p] = (
                -GROUP_PREF * p[2]
                + half * p[1]
                + depth * p[0]
                + column * p[3]
            )
    left = 4 * (len(pieces) - KGROUPS * 4)
    rounds = []
    while left:
        now = len(rounds)
        row = [[None] * 4 for _ in range(3)]
        for link in LINK_ORDER:
            for place in range(4):
                best, best_worth = None, -1e18
                for p in pieces:
                    if ready[place][p] <= now:
                        to, there = moved(link, place, p)
                        if not taken[to][there]:
                            w = worth[link, there]
                            if link == 2:
                                w += CHAIN_PREF * there[1] * (3 - to)
                            if w > best_worth:
                                best, best_worth = (p, to, there), w
                if best is not None:
                    p, to, there = best
                    taken[to][there] = True
                    ready[to][there] = now + LAG
                    left -= 1
                    row[link][place] = p
        rounds.append(row)
    return rounds, ready


def arrivals_of(rounds):
    result = []
    for row in rounds:
        got = [[None] * 4 for _ in range(3)]
        for link in range(3):
            for place in range(4):
                if row[link][place] is not None:
                    to, there = moved(link, place, row[link][place])
                    got[link][to] = there
        result.append(got)
    return result


def group_rounds(ready):
    mine, both = {}, {}
    for dy in range(4):
        for h in range(2):
            for k in range(KGROUPS):
                mine[dy, h, k] = max(ready[place][dy, h, k, r] for place in range(4) for r in range(4))
    for dy, h, k in mine:
        both[dy, h, k] = max(mine[dy, h, k], mine[(4 - dy) % 4, h, k] + RELAY_LAG)
        if (dy, h) == (0, 0):
            both[dy, h, k] = 0
    return mine, both


def kernel(
    n_dp,
    lat_ref,
    wq_ref,
    wo_ref,
    text_ref,
    counts_ref,
    conds_ref,
    guide_ref,
    scale_ref,
    shift_ref,
    out_ref,
    wq,
    wo,
    x_buf,
    text,
    q_acc,
    att,
    acc,
    send_sem,
    recv_sem,
    sib_sem,
    local_sem,
):
    rounds, ready = make_rounds()
    arrivals = arrivals_of(rounds)
    n_rounds = len(rounds)
    dp, fs = lax.axis_index("dp"), lax.axis_index("fsdp")
    core, x_at, z_lo = dp % 2, (dp // 2) % 4, dp // 8
    y_at, z_hi = fs // 2, fs % 2
    sign = 1 - 2 * core
    column = (4 + sign * x_at) % 4
    place = z_lo + core * (3 - 2 * z_lo)
    z_next = (z_hi * 4 + z_lo + 8 + sign) % 8
    z_prev = (z_hi * 4 + z_lo + 8 - sign) % 8
    targets = (
        (z_lo * 8 + ((x_at + 4 + sign) % 4) * 2 + core, fs),
        (dp, ((y_at + 4 + sign) % 4) * 2 + z_hi),
        ((z_next % 4) * 8 + x_at * 2 + core, y_at * 2 + z_next // 4),
    )
    sources = (
        (z_lo * 8 + ((x_at + 4 - sign) % 4) * 2 + core, fs),
        (dp, ((y_at + 4 - sign) % 4) * 2 + z_hi),
        ((z_prev % 4) * 8 + x_at * 2 + core, y_at * 2 + z_prev // 4),
    )
    sibling = (dp + sign, fs)

    fetches = [
        pltpu.make_async_copy(wq_ref, wq.at[fs], local_sem.at[0]),
        pltpu.make_async_copy(wo_ref, wo.at[fs], local_sem.at[1]),
        pltpu.make_async_copy(lat_ref, x_buf, local_sem.at[2]),
        pltpu.make_async_copy(text_ref, text, local_sem.at[3]),
    ]
    for fetch in fetches:
        fetch.start()
    barrier = pltpu.get_barrier_semaphore()
    for other in sources + (sibling,):
        pl.semaphore_signal(barrier, inc=1, device_id=other, device_id_type=MESH)
    pl.semaphore_wait(barrier, 4)
    fetches[0].wait()
    fetches[1].wait()

    shards = {
        (dy, h): ((y_at + 4 - sign * dy) % 4) * 2 + (z_hi + h) % 2 for dy in range(4) for h in range(2)
    }
    columns = [(column + 4 - r) % 4 for r in range(4)]
    row_at = (
        [core * 256 + c * 64 for c in columns],
        [core * 128 + c * 32 for c in columns],
    )

    def pick(options, of):
        keyed = {}
        for p, piece in options.items():
            key, value = of(piece)
            keyed.setdefault(key, (value, []))[1].append(p)
        groups = list(keyed.values())
        result = groups[-1][0]
        for value, places in groups[:-1]:
            here = functools.reduce(jnp.logical_or, [place == p for p in places])
            result = jnp.where(here, value, result)
        return result

    def slot(options, weight):
        shard = pick(options, lambda p: (p[:2], shards[p[:2]]))
        row = pick(options, lambda p: (p[3], row_at[weight][p[3]]))
        half = pick(options, lambda p: (p[2] % 2, p[2] % 2))
        if weight == 0:
            return wq.at[
                shard,
                pl.ds(pl.multiple_of(row, 64), 64),
                pl.ds(pl.multiple_of(half * 1024, 1024), 1024),
            ]
        return wo.at[
            shard,
            pl.ds(pl.multiple_of(row, 32), 32),
            pl.ds(pl.multiple_of(half * 2048, 2048), 2048),
        ]

    def for_places(row, action):
        for weight in range(2):
            options = {
                p: row[p] for p in range(4) if row[p] is not None and row[p][2] // 2 == weight
            }
            if not options:
                continue
            if len(options) == 4:
                action(options, weight)
            else:
                here = functools.reduce(jnp.logical_or, [place == p for p in options])
                pl.when(here)(functools.partial(action, options, weight))

    def link_copy(link, step, options, weight):
        ref = slot(options, weight)
        return pltpu.make_async_remote_copy(
            src_ref=ref,
            dst_ref=ref,
            send_sem=send_sem.at[link],
            recv_sem=recv_sem.at[link * n_rounds + step],
            device_id=targets[link],
            device_id_type=MESH,
        )

    def half_group(dy, h, k, of_core):
        shard = shards[dy, h]
        if k < 2:
            rows = pl.ds(pl.multiple_of(of_core * 256, 256), 256)
            return wq.at[shard, rows, pl.ds(k * 1024, 1024)], sib_sem.at[k * 8 + shard]
        rows = pl.ds(pl.multiple_of(of_core * 128, 128), 128)
        return wo.at[shard, rows, pl.ds((k - 2) * 2048, 2048)], sib_sem.at[k * 8 + shard]

    def relay(dy, h, k):
        ref, sem = half_group(dy, h, k, core)
        pltpu.make_async_remote_copy(
            src_ref=ref,
            dst_ref=ref,
            send_sem=send_sem.at[3],
            recv_sem=sem,
            device_id=sibling,
            device_id_type=MESH,
        ).start()

    def wait_sibling(dy, h, k):
        if (dy, h) != (0, 0):
            ref, sem = half_group(dy, h, k, 1 - core)
            pltpu.make_async_copy(ref, ref, sem).wait()

    def wait_sent(sem, ref):
        pltpu.make_async_copy(ref, ref, sem).wait()

    mine, both = group_rounds(ready)
    order = sorted(shards, key=lambda s: (both[s + (3,)], s))
    places_of = []
    for shard in range(8):
        back = (sign * (y_at - shard // 2) + 4) % 4
        key = back * 2 + (z_hi + shard) % 2
        at = jnp.int32(0)
        for i, (dy, h) in enumerate(order):
            at = jnp.where(key == dy * 2 + h, i, at)
        places_of.append(at * 256)

    def query_task(first, dy, h, k):
        wait_sibling(dy, h, k)
        shard = shards[dy, h]
        at = pl.ds(k * 1024, 1024)
        part = jnp.dot(
            x_buf[:, pl.ds(pl.multiple_of(shard * 512, 512), 512)],
            wq[shard, :, at],
            preferred_element_type=jnp.float32,
        )
        if first:
            q_acc[:, at] = part
        else:
            q_acc[:, at] += part

    def attend_task(shard):
        scored = []
        for p in range(2):
            head = shard * 2 + p
            queries = q_acc[:, head * HDIM : (head + 1) * HDIM].astype(jnp.bfloat16)
            for cond in range(4):
                scores = lax.dot_general(
                    queries,
                    text[cond, :, head * HDIM : (head + 1) * HDIM],
                    (((1,), (1,)), ((), ())),
                    preferred_element_type=jnp.float32,
                )
                scored.append((p, cond, scores))
        weighed = []
        for p, cond, scores in scored:
            peak = jnp.max(scores, axis=-1, keepdims=True)
            expd = jnp.exp2((scores - peak) * (math.log2(math.e) / math.sqrt(HDIM)))
            probs = (expd * (1.0 / jnp.sum(expd, axis=-1, keepdims=True))).astype(jnp.bfloat16)
            weighed.append((p, cond, probs))
        for p, cond, probs in weighed:
            value_at = 2048 + (shard * 2 + p) * HDIM
            result = jnp.dot(
                probs, text[cond, :, value_at : value_at + HDIM], preferred_element_type=jnp.float32
            )
            at = pl.ds(pl.multiple_of(places_of[shard] + p * HDIM, HDIM), HDIM)
            att[pl.ds(cond * 128, 128), at] = result.astype(jnp.bfloat16)

    def out_task(low, high, start, width, k):
        if start == (k - 2) * 2048:
            for dy, h in order[low:high]:
                wait_sibling(dy, h, k)
        at = pl.ds(start, width)
        part = jnp.dot(
            att[:, low * 256 : high * 256],
            jnp.concatenate([wo[shards[s], :, at] for s in order[low:high]], axis=0),
            preferred_element_type=jnp.float32,
        )
        if low == 0:
            base = x_buf[:, at].astype(jnp.float32)
            acc[:, at] = part + jnp.concatenate([base] * 4, axis=0)
        else:
            acc[:, at] += part

    tasks = []
    for k in range(2):
        stage = 2 * k
        for i, s in enumerate(sorted(shards, key=lambda s: (both[s + (k,)], s))):
            call = functools.partial(query_task, i == 0, *s, k)
            tasks.append((stage, -1, both[s + (k,)], QUERY_US, call))
        for shard in range(4 * k, 4 * k + 4):
            call = functools.partial(attend_task, shard)
            tasks.append((stage + 1, stage, 0, ATTEND_US, call))
    cut = 8 - LAST_SHARDS
    when = max(both[s + (2,)] for s in order)
    for start in range(0, 2048, 256):
        call = functools.partial(out_task, 0, 8, start, 256, 2)
        tasks.append((4, 3, when, OUT_US, call))
    for low, high, stage in ((0, cut, 5), (cut, 8, 6)):
        when = max(both[s + (3,)] for s in order[low:high])
        for start in range(2048, 4096, 512):
            call = functools.partial(out_task, low, high, start, 512, 3)
            tasks.append((stage, stage - 1, when, OUT_US * 2 * (high - low) / 8, call))

    def next_task(step, budget):
        for i, (stage, after, when, cost, call) in enumerate(tasks):
            if when <= step and cost <= budget and not any(t[0] <= after for t in tasks):
                if stage < 4 or i == 0:
                    tasks.pop(i)
                    return cost, call
        return None

    fetched = False
    for step in range(n_rounds + LAG):
        came = step - LAG
        if came >= 0:
            for link in range(3):
                for_places(
                    arrivals[came][link],
                    lambda options, weight, link=link: link_copy(
                        link, came, options, weight
                    ).wait_recv(),
                )
        if step < n_rounds:
            for link in range(3):
                for_places(
                    rounds[step][link],
                    lambda options, weight, link=link: link_copy(
                        link, step, options, weight
                    ).start(),
                )
        for group in mine:
            if mine[group] == step and step > 0:
                relay(*group)
        if step >= 1:
            if not fetched:
                fetches[2].wait()
                fetches[3].wait()
                fetched = True
            budget = ROUND_US
            while (found := next_task(step, budget)) is not None:
                budget -= found[0]
                found[1]()
    while tasks:
        next_task(1 << 20, 1 << 20)[1]()

    @pl.loop(0, 4)
    def _(member):
        latent = dp * 4 + member
        count = counts_ref[latent]
        total = jnp.int32(0)
        weights = [jnp.int32(0)] * 4
        for s in range(4):
            weight = jnp.where(s < count, guide_ref[s], 0)
            total = total + weight
            cond = conds_ref[s, latent]
            weights = [w + jnp.where(cond == c, weight, 0) for c, w in enumerate(weights)]
        share = 1.0 / jnp.full((32, 1), total.astype(jnp.float32))
        scale = 1.0 + scale_ref[pl.ds(member, 1), :]
        shift = shift_ref[pl.ds(member, 1), :]
        start = pl.multiple_of(member * 32, 32)
        rows = [pl.ds(pl.multiple_of(c * 128 + start, 32), 32) for c in range(4)]
        spans = [slice(j, j + 128) for j in range(0, 4096, 128)]
        centers, gains = [], []
        for c in range(4):
            summed = jnp.zeros((32, 128), jnp.float32)
            for at in spans:
                summed += acc[rows[c], at]
            centers.append(jnp.sum(summed, axis=-1, keepdims=True) / 4096)
        for c in range(4):
            summed = jnp.zeros((32, 128), jnp.float32)
            for at in spans:
                moved_h = acc[rows[c], at] - centers[c]
                summed += moved_h * moved_h
            spread = jnp.sum(summed, axis=-1, keepdims=True) / 4096
            gains.append(lax.rsqrt(spread + 1e-06) * (weights[c].astype(jnp.float32) * share))
        for at in spans:
            numer = jnp.zeros((32, 128), jnp.float32)
            for c in range(4):
                numer += (acc[rows[c], at] - centers[c]) * gains[c]
            combined = numer.astype(jnp.bfloat16).astype(jnp.float32)
            out_ref[pl.ds(start, 32), at] = (
                combined * scale[:, at] + shift[:, at]
            ).astype(jnp.bfloat16)

    for link in range(3):
        sends = [sum(row[link][p] is not None for row in rounds) for p in range(4)]
        for many in sorted(set(sends)):
            here = functools.reduce(
                jnp.logical_or, [place == p for p in range(4) if sends[p] == many]
            )
            pl.when(here)(
                functools.partial(wait_sent, send_sem.at[link], acc.at[pl.ds(0, many * 8)])
            )
    wait_sent(send_sem.at[3], wq.at[pl.ds(0, 7)])


def on_device(
    n_dp,
    latents,
    w_query,
    w_out,
    text_cache,
    branch_counts,
    branch_conds,
    guide_weights,
    mod_scale,
    mod_shift,
):
    members, rows_here, width = latents.shape
    rows = members * rows_here
    n_rounds = len(make_rounds()[0])
    anywhere = pl.BlockSpec(memory_space=pl.ANY)
    in_vmem = pl.BlockSpec(memory_space=pltpu.VMEM)
    in_smem = pl.BlockSpec(memory_space=pltpu.SMEM)
    mixed = pl.pallas_call(
        functools.partial(kernel, n_dp),
        out_shape=jax.ShapeDtypeStruct((rows, width), jnp.bfloat16),
        in_specs=[anywhere] * 4 + [in_smem] * 3 + [in_vmem] * 2,
        out_specs=in_vmem,
        scratch_shapes=[
            pltpu.VMEM((8, 512, 2048), jnp.bfloat16),
            pltpu.VMEM((8, 256, 4096), jnp.bfloat16),
            pltpu.VMEM((rows, width), jnp.bfloat16),
            pltpu.VMEM(text_cache.shape, jnp.bfloat16),
            pltpu.VMEM((rows, 2048), jnp.float32),
            pltpu.VMEM((4 * rows, 2048), jnp.bfloat16),
            pltpu.VMEM((4 * rows, width), jnp.float32),
            pltpu.SemaphoreType.DMA((4,)),
            pltpu.SemaphoreType.DMA((3 * n_rounds,)),
            pltpu.SemaphoreType.DMA((8 * KGROUPS,)),
            pltpu.SemaphoreType.DMA((4,)),
        ],
        compiler_params=pltpu.CompilerParams(
            collective_id=0, has_side_effects=True, vmem_limit_bytes=58 * 2**20
        ),
        name="gather_and_attend",
    )(
        latents.reshape(rows, width),
        w_query,
        w_out,
        text_cache,
        branch_counts,
        branch_conds.T,
        guide_weights,
        mod_scale,
        mod_shift,
    )
    return mixed.reshape(members, rows_here, width)


def solution(mesh):
    return jax.shard_map(
        functools.partial(on_device, mesh.shape["dp"]),
        mesh=mesh,
        in_specs=(
            P("dp", "fsdp", None),
            P("fsdp", None),
            P("fsdp", None),
            P(),
            P(),
            P(),
            P(),
            P("dp", None),
            P("dp", None),
        ),
        out_specs=P("dp", "fsdp", None),
        check_vma=False,
    )
```

```python
import functools
import math

import jax
import jax.numpy as jnp
from jax import lax
from jax.experimental import pallas as pl
from jax.experimental.pallas import tpu as pltpu
from jax.sharding import PartitionSpec as P

HDIM = 128
MESH = pl.DeviceIdType.MESH
LAG = 3
KGROUPS = 4
RELAY_LAG = (2, 2, 2, 1)
ROUNDS = (
    (-1, -1, -1, -1, 10, 8, 11, 9, -1, -1, -1, 3),
    (-1, -1, -1, -1, 3, 0, 3, 11, -1, -1, -1, 2),
    (-1, -1, -1, -1, 1, 4, 1, 7, -1, -1, -1, 11),
    (19, 40, 43, 41, 42, 40, 43, 41, 19, -1, -1, 41),
    (35, 32, 35, 43, 19, 6, 35, 14, 18, -1, 35, 43),
    (33, 36, 33, 39, 6, 3, 6, 39, 42, 36, 33, 9),
    (27, 72, 40, 73, 16, 11, 40, 6, 57, 19, 75, 42),
    (59, 19, 67, 46, 5, 33, 67, 0, 51, 18, 67, 1),
    (25, 38, 38, 71, 34, 38, 75, 40, 34, 42, 34, 39),
    (74, 73, 72, 36, 11, 43, 19, 38, 58, 57, 19, 38),
    (38, 65, 99, 67, 37, 65, 18, 47, 48, 65, 99, 67),
    (55, 70, 107, 68, 18, 51, 39, 74, 17, 70, 107, 68),
    (48, 58, 51, 19, 48, 73, 51, 34, 55, 58, 51, 37),
    (39, 97, 96, 99, 39, 35, 73, 70, 69, 66, 65, 99),
    (75, 83, 19, 79, 84, 83, 5, 71, 56, 17, 18, 69),
    (80, 105, 71, 16, 80, 18, 58, 51, 53, 59, 48, 66),
    (71, 98, 105, 96, 38, 69, 66, 66, 49, 55, 105, 102),
    (116, 71, 73, 76, 33, 80, 37, 12, 116, 80, 58, 103),
    (112, 106, 90, 48, 82, 53, 17, 83, 82, 115, 50, 83),
    (72, 99, 55, 83, 118, 49, 55, 79, 118, 53, 55, 15),
    (85, 116, 80, 77, 119, 68, 80, 58, 119, 116, 104, 44),
    (67, 67, 91, 115, 117, 116, 91, 49, 114, 82, 57, 115),
    (43, 107, 87, 55, 73, 81, 87, 50, 22, 118, 53, 73),
    (60, 101, 116, 103, 31, 117, 81, 55, 23, 100, 116, 104),
    (99, 53, 88, 112, 74, 20, 123, 90, 60, 20, 88, 107),
    (40, 85, 53, 53, 89, 55, 82, 82, 26, 22, 119, 78),
    (23, 102, 100, 116, 75, 58, 119, 116, 63, 21, 118, 116),
    (96, 60, 59, 100, 15, 52, 89, 88, 24, 60, 27, 106),
    (94, 26, 27, 88, 94, 15, 53, 119, 121, 86, 22, 114),
    (107, 90, 123, 20, 58, 14, 15, 122, 94, 63, 59, 119),
    (86, 24, 60, 120, 47, 63, 121, 52, 122, 26, 56, 118),
    (126, 61, 101, 27, 126, 47, 60, 54, 126, 103, 85, 117),
    (95, 91, 47, 122, 13, 46, 47, 59, 120, 94, 60, 46),
    (79, 122, 61, 111, 56, 95, 13, 121, 89, 122, 61, 75),
    (127, 95, 92, 44, 14, 79, 92, 78, 31, 126, 92, 13),
    (92, 79, 94, -1, 45, 12, 79, 77, 30, 78, 63, 12),
    (47, 127, 45, 61, 79, 61, 45, 61, 45, 127, 94, -1),
    (124, 111, 124, -1, 76, 78, 126, 92, 29, 31, 126, -1),
    (77, 76, 111, -1, 77, -1, 78, -1, 28, 76, 95, -1),
    (-1, 124, -1, -1, -1, -1, 77, 93, -1, -1, 127, -1),
    (-1, 108, 31, -1, -1, -1, -1, 124, -1, 29, 30, 126),
    (-1, -1, -1, -1, -1, -1, -1, -1, -1, -1, 31, -1),
    (-1, -1, -1, -1, -1, -1, -1, 125, -1, -1, -1, -1),
)
ROUND_US = 1.5
QUERY_US, ATTEND_US, OUT_US, STATS_US = 0.27, 0.72, 0.72, 0.3
LAST_SHARDS = 3


def moved(link, place, piece):
    dy, h, k, r = piece
    if link == 0:
        return place, (dy, h, k, (r + 1) % 4)
    if link == 1:
        return place, ((dy + 1) % 4, h, k, r)
    if place < 3:
        return place + 1, piece
    return 0, (dy, 1 - h, k, r)


def named(number):
    return None if number < 0 else (number // 32, number // 16 % 2, number // 4 % 4, number % 4)


def make_rounds():
    rounds = [[[named(row[link * 4 + p]) for p in range(4)] for link in range(3)] for row in ROUNDS]
    ready = [{named(n): 0 for n in range(16)} for _ in range(4)]
    for now, row in enumerate(rounds):
        for link in range(3):
            for place in range(4):
                piece = row[link][place]
                if piece is not None:
                    to, there = moved(link, place, piece)
                    assert ready[place][piece] <= now and there not in ready[to]
                    ready[to][there] = now + LAG
    assert all(len(r) == 128 for r in ready)
    return rounds, ready


def arrivals_of(rounds):
    result = []
    for row in rounds:
        got = [[None] * 4 for _ in range(3)]
        for link in range(3):
            for place in range(4):
                if row[link][place] is not None:
                    to, there = moved(link, place, row[link][place])
                    got[link][to] = there
        result.append(got)
    return result


def group_rounds(ready):
    mine, both = {}, {}
    for dy in range(4):
        for h in range(2):
            for k in range(KGROUPS):
                mine[dy, h, k] = max(ready[place][dy, h, k, r] for place in range(4) for r in range(4))
    for dy, h, k in mine:
        both[dy, h, k] = max(mine[dy, h, k], mine[(4 - dy) % 4, h, k] + RELAY_LAG[k])
        if (dy, h) == (0, 0):
            both[dy, h, k] = 0
    return mine, both


def kernel(
    n_dp,
    lat_ref,
    wq_ref,
    wo_ref,
    text_ref,
    counts_ref,
    conds_ref,
    guide_ref,
    scale_ref,
    shift_ref,
    out_ref,
    wq,
    wo,
    x_buf,
    text,
    q_acc,
    att,
    acc,
    half_center,
    half_spread,
    send_sem,
    recv_sem,
    sib_sem,
    local_sem,
):
    rounds, ready = make_rounds()
    arrivals = arrivals_of(rounds)
    n_rounds = len(rounds)
    dp, fs = lax.axis_index("dp"), lax.axis_index("fsdp")
    core, x_at, z_lo = dp % 2, (dp // 2) % 4, dp // 8
    y_at, z_hi = fs // 2, fs % 2
    sign = 1 - 2 * core
    column = (4 + sign * x_at) % 4
    place = z_lo + core * (3 - 2 * z_lo)
    z_next = (z_hi * 4 + z_lo + 8 + sign) % 8
    z_prev = (z_hi * 4 + z_lo + 8 - sign) % 8
    targets = (
        (z_lo * 8 + ((x_at + 4 + sign) % 4) * 2 + core, fs),
        (dp, ((y_at + 4 + sign) % 4) * 2 + z_hi),
        ((z_next % 4) * 8 + x_at * 2 + core, y_at * 2 + z_next // 4),
    )
    sources = (
        (z_lo * 8 + ((x_at + 4 - sign) % 4) * 2 + core, fs),
        (dp, ((y_at + 4 - sign) % 4) * 2 + z_hi),
        ((z_prev % 4) * 8 + x_at * 2 + core, y_at * 2 + z_prev // 4),
    )
    sibling = (dp + sign, fs)

    fetches = [
        pltpu.make_async_copy(wq_ref, wq.at[fs], local_sem.at[0]),
        pltpu.make_async_copy(wo_ref, wo.at[fs], local_sem.at[1]),
        pltpu.make_async_copy(lat_ref, x_buf, local_sem.at[2]),
        pltpu.make_async_copy(text_ref, text, local_sem.at[3]),
    ]
    for fetch in fetches[:3]:
        fetch.start()
    barrier = pltpu.get_barrier_semaphore()
    for other in sources + (sibling,):
        pl.semaphore_signal(barrier, inc=1, device_id=other, device_id_type=MESH)
    pl.semaphore_wait(barrier, 4)
    fetches[0].wait()
    out_fetched = False

    shards = {
        (dy, h): ((y_at + 4 - sign * dy) % 4) * 2 + (z_hi + h) % 2 for dy in range(4) for h in range(2)
    }
    columns = [(column + 4 - r) % 4 for r in range(4)]
    row_at = (
        [core * 256 + c * 64 for c in columns],
        [core * 128 + c * 32 for c in columns],
    )

    def pick(options, of):
        keyed = {}
        for p, piece in options.items():
            key, value = of(piece)
            keyed.setdefault(key, (value, []))[1].append(p)
        groups = list(keyed.values())
        result = groups[-1][0]
        for value, places in groups[:-1]:
            here = functools.reduce(jnp.logical_or, [place == p for p in places])
            result = jnp.where(here, value, result)
        return result

    def slot(options, weight):
        shard = pick(options, lambda p: (p[:2], shards[p[:2]]))
        row = pick(options, lambda p: (p[3], row_at[weight][p[3]]))
        half = pick(options, lambda p: (p[2] % 2, p[2] % 2))
        if weight == 0:
            return wq.at[
                shard,
                pl.ds(pl.multiple_of(row, 64), 64),
                pl.ds(pl.multiple_of(half * 1024, 1024), 1024),
            ]
        return wo.at[
            shard,
            pl.ds(pl.multiple_of(row, 32), 32),
            pl.ds(pl.multiple_of(half * 2048, 2048), 2048),
        ]

    def for_places(row, action):
        for weight in range(2):
            options = {
                p: row[p] for p in range(4) if row[p] is not None and row[p][2] // 2 == weight
            }
            if not options:
                continue
            if len(options) == 4:
                action(options, weight)
            else:
                here = functools.reduce(jnp.logical_or, [place == p for p in options])
                pl.when(here)(functools.partial(action, options, weight))

    def link_copy(link, step, options, weight):
        ref = slot(options, weight)
        return pltpu.make_async_remote_copy(
            src_ref=ref,
            dst_ref=ref,
            send_sem=send_sem.at[link],
            recv_sem=recv_sem.at[link * n_rounds + step],
            device_id=targets[link],
            device_id_type=MESH,
        )

    def half_group(dy, h, k, of_core):
        shard = shards[dy, h]
        if k < 2:
            rows = pl.ds(pl.multiple_of(of_core * 256, 256), 256)
            return wq.at[shard, rows, pl.ds(k * 1024, 1024)], sib_sem.at[k * 8 + shard]
        rows = pl.ds(pl.multiple_of(of_core * 128, 128), 128)
        return wo.at[shard, rows, pl.ds((k - 2) * 2048, 2048)], sib_sem.at[k * 8 + shard]

    def relay_piece(options, weight):
        ref = slot(options, weight)
        shard = pick(options, lambda p: (p[:2], shards[p[:2]]))
        pltpu.make_async_remote_copy(
            src_ref=ref,
            dst_ref=ref,
            send_sem=send_sem.at[3],
            recv_sem=sib_sem.at[3 * 8 + shard],
            device_id=sibling,
            device_id_type=MESH,
        ).start()

    def relay(dy, h, k):
        ref, sem = half_group(dy, h, k, core)
        pltpu.make_async_remote_copy(
            src_ref=ref,
            dst_ref=ref,
            send_sem=send_sem.at[3],
            recv_sem=sem,
            device_id=sibling,
            device_id_type=MESH,
        ).start()

    def wait_sibling(dy, h, k):
        if (dy, h) != (0, 0):
            ref, sem = half_group(dy, h, k, 1 - core)
            pltpu.make_async_copy(ref, ref, sem).wait()

    def wait_sent(sem, ref):
        pltpu.make_async_copy(ref, ref, sem).wait()

    mine, both = group_rounds(ready)
    order = sorted(shards, key=lambda s: (both[s + (3,)], s))
    places_of = []
    for shard in range(8):
        back = (sign * (y_at - shard // 2) + 4) % 4
        key = back * 2 + (z_hi + shard) % 2
        at = jnp.int32(0)
        for i, (dy, h) in enumerate(order):
            at = jnp.where(key == dy * 2 + h, i, at)
        places_of.append(at * 256)

    def query_task(first, dy, h, k):
        wait_sibling(dy, h, k)
        shard = shards[dy, h]
        at = pl.ds(k * 1024, 1024)
        part = jnp.dot(
            x_buf[:, pl.ds(pl.multiple_of(shard * 512, 512), 512)],
            wq[shard, :, at],
            preferred_element_type=jnp.float32,
        )
        if first:
            q_acc[:, at] = part
        else:
            q_acc[:, at] += part

    def attend_task(shard):
        scored = []
        for p in range(2):
            head = shard * 2 + p
            queries = q_acc[:, head * HDIM : (head + 1) * HDIM].astype(jnp.bfloat16)
            for cond in range(4):
                scores = lax.dot_general(
                    queries,
                    text[cond, :, head * HDIM : (head + 1) * HDIM],
                    (((1,), (1,)), ((), ())),
                    preferred_element_type=jnp.float32,
                )
                scored.append((p, cond, scores))
        weighed = []
        for p, cond, scores in scored:
            peak = jnp.max(scores, axis=-1, keepdims=True)
            expd = jnp.exp2((scores - peak) * (math.log2(math.e) / math.sqrt(HDIM)))
            probs = (expd * (1.0 / jnp.sum(expd, axis=-1, keepdims=True))).astype(jnp.bfloat16)
            weighed.append((p, cond, probs))
        for p, cond, probs in weighed:
            value_at = 2048 + (shard * 2 + p) * HDIM
            result = jnp.dot(
                probs, text[cond, :, value_at : value_at + HDIM], preferred_element_type=jnp.float32
            )
            at = pl.ds(pl.multiple_of(places_of[shard] + p * HDIM, HDIM), HDIM)
            att[pl.ds(cond * 128, 128), at] = result.astype(jnp.bfloat16)

    def out_task(low, high, start, width, k):
        if start == (k - 2) * 2048:
            for dy, h in order[low:high]:
                wait_sibling(dy, h, k)
        at = pl.ds(start, width)
        part = jnp.dot(
            att[:, low * 256 : high * 256],
            jnp.concatenate([wo[shards[s], :, at] for s in order[low:high]], axis=0),
            preferred_element_type=jnp.float32,
        )
        if low == 0:
            base = x_buf[:, at].astype(jnp.float32)
            acc[:, at] = part + jnp.concatenate([base] * 4, axis=0)
        else:
            acc[:, at] += part

    def stats_task(start):
        for low in range(start, start + 64, 32):
            rows = slice(low, low + 32)
            summed = jnp.zeros((32, 128), jnp.float32)
            for j in range(0, 2048, 128):
                summed += acc[rows, j : j + 128]
            center = jnp.sum(summed, axis=-1, keepdims=True) / 2048
            summed = jnp.zeros((32, 128), jnp.float32)
            for j in range(0, 2048, 128):
                moved_h = acc[rows, j : j + 128] - center
                summed += moved_h * moved_h
            half_center[rows] = jnp.broadcast_to(center, (32, 128))
            half_spread[rows] = summed

    tasks = []
    for k in range(2):
        stage = 2 * k
        for i, s in enumerate(sorted(shards, key=lambda s: (both[s + (k,)], s))):
            call = functools.partial(query_task, i == 0, *s, k)
            tasks.append((stage, -1, both[s + (k,)], QUERY_US, call))
        for shard in range(4 * k, 4 * k + 4):
            call = functools.partial(attend_task, shard)
            tasks.append((stage + 1, stage, 0, ATTEND_US, call))
    cut = 8 - LAST_SHARDS
    when = max(both[s + (2,)] for s in order)
    for start in range(0, 2048, 256):
        call = functools.partial(out_task, 0, 8, start, 256, 2)
        tasks.append((4, 3, when, OUT_US, call))
    for start in range(0, 512, 64):
        tasks.append((5, 4, 0, STATS_US, functools.partial(stats_task, start)))
    for low, high, stage in ((0, cut, 6), (cut, 8, 7)):
        when = max(both[s + (3,)] for s in order[low:high])
        for start in range(2048, 4096, 512):
            call = functools.partial(out_task, low, high, start, 512, 3)
            after = 4 if stage == 6 else 6
            tasks.append((stage, after, when, OUT_US * 2 * (high - low) / 8, call))

    def next_task(step, budget):
        for i, (stage, after, when, cost, call) in enumerate(tasks):
            if when <= step and cost <= budget and not any(t[0] <= after for t in tasks):
                tasks.pop(i)
                return cost, call
        return None

    fetched = False
    for step in range(n_rounds + LAG):
        came = step - LAG
        if came >= 0:
            for link in range(3):
                for_places(
                    arrivals[came][link],
                    lambda options, weight, link=link: link_copy(
                        link, came, options, weight
                    ).wait_recv(),
                )
        if step < n_rounds:
            if not out_fetched and any(p is not None and p[2] > 1 for got in rounds[step] for p in got):
                fetches[1].wait()
                out_fetched = True
            for link in range(3):
                for_places(
                    rounds[step][link],
                    lambda options, weight, link=link: link_copy(
                        link, step, options, weight
                    ).start(),
                )
            if step == 0:
                fetches[3].start()
        if came >= 0:
            for link in range(3):
                last_group = [p if p is not None and p[2] == 3 else None for p in arrivals[came][link]]
                for_places(last_group, relay_piece)
        for group in mine:
            if mine[group] == step and step > 0 and group[2] < 3:
                relay(*group)
        if step >= 1:
            if not fetched:
                fetches[2].wait()
                fetches[3].wait()
                fetched = True
            budget = ROUND_US
            while (found := next_task(step, budget)) is not None:
                budget -= found[0]
                found[1]()
    while tasks:
        next_task(1 << 20, 1 << 20)[1]()

    @pl.loop(0, 4)
    def _(member):
        latent = dp * 4 + member
        count = counts_ref[latent]
        total = jnp.int32(0)
        weights = [jnp.int32(0)] * 4
        for s in range(4):
            weight = jnp.where(s < count, guide_ref[s], 0)
            total = total + weight
            cond = conds_ref[s, latent]
            weights = [w + jnp.where(cond == c, weight, 0) for c, w in enumerate(weights)]
        share = 1.0 / jnp.full((32, 1), total.astype(jnp.float32))
        scale = 1.0 + scale_ref[pl.ds(member, 1), :]
        shift = shift_ref[pl.ds(member, 1), :]
        start = pl.multiple_of(member * 32, 32)
        rows = [pl.ds(pl.multiple_of(c * 128 + start, 32), 32) for c in range(4)]
        spans = [slice(j, j + 128) for j in range(0, 4096, 128)]
        gains, offset = [], jnp.zeros((32, 1), jnp.float32)
        for c in range(4):
            pivot = half_center[rows[c]]
            summed, squares = jnp.zeros((32, 128), jnp.float32), half_spread[rows[c]]
            for at in spans[16:]:
                moved_h = acc[rows[c], at] - pivot
                summed += moved_h
                squares += moved_h * moved_h
            shift_c = jnp.sum(summed, axis=-1, keepdims=True) / 4096
            spread = jnp.sum(squares, axis=-1, keepdims=True) / 4096 - shift_c * shift_c
            spread = jnp.maximum(spread, 0.0)
            gain = lax.rsqrt(spread + 1e-06) * (weights[c].astype(jnp.float32) * share)
            gains.append(gain)
            offset += (pivot[:, :1] + shift_c) * gain
        for at in spans:
            numer = -offset
            for c in range(4):
                numer += acc[rows[c], at] * gains[c]
            combined = numer.astype(jnp.bfloat16).astype(jnp.float32)
            out_ref[pl.ds(start, 32), at] = (
                combined * scale[:, at] + shift[:, at]
            ).astype(jnp.bfloat16)

    for link in range(3):
        sends = [sum(row[link][p] is not None for row in rounds) for p in range(4)]
        for many in sorted(set(sends)):
            here = functools.reduce(
                jnp.logical_or, [place == p for p in range(4) if sends[p] == many]
            )
            pl.when(here)(
                functools.partial(wait_sent, send_sem.at[link], acc.at[pl.ds(0, many * 8)])
            )
    wait_sent(send_sem.at[3], wq.at[pl.ds(0, 7)])


def on_device(
    n_dp,
    latents,
    w_query,
    w_out,
    text_cache,
    branch_counts,
    branch_conds,
    guide_weights,
    mod_scale,
    mod_shift,
):
    members, rows_here, width = latents.shape
    rows = members * rows_here
    n_rounds = len(make_rounds()[0])
    anywhere = pl.BlockSpec(memory_space=pl.ANY)
    in_vmem = pl.BlockSpec(memory_space=pltpu.VMEM)
    in_smem = pl.BlockSpec(memory_space=pltpu.SMEM)
    mixed = pl.pallas_call(
        functools.partial(kernel, n_dp),
        out_shape=jax.ShapeDtypeStruct((rows, width), jnp.bfloat16),
        in_specs=[anywhere] * 4 + [in_smem] * 3 + [in_vmem] * 2,
        out_specs=in_vmem,
        scratch_shapes=[
            pltpu.VMEM((8, 512, 2048), jnp.bfloat16),
            pltpu.VMEM((8, 256, 4096), jnp.bfloat16),
            pltpu.VMEM((rows, width), jnp.bfloat16),
            pltpu.VMEM(text_cache.shape, jnp.bfloat16),
            pltpu.VMEM((rows, 2048), jnp.float32),
            pltpu.VMEM((4 * rows, 2048), jnp.bfloat16),
            pltpu.VMEM((4 * rows, width), jnp.float32),
            pltpu.VMEM((4 * rows, 128), jnp.float32),
            pltpu.VMEM((4 * rows, 128), jnp.float32),
            pltpu.SemaphoreType.DMA((4,)),
            pltpu.SemaphoreType.DMA((3 * n_rounds,)),
            pltpu.SemaphoreType.DMA((8 * KGROUPS,)),
            pltpu.SemaphoreType.DMA((4,)),
        ],
        compiler_params=pltpu.CompilerParams(
            collective_id=0, has_side_effects=True, vmem_limit_bytes=58 * 2**20
        ),
        name="gather_and_attend",
    )(
        latents.reshape(rows, width),
        w_query,
        w_out,
        text_cache,
        branch_counts,
        branch_conds.T,
        guide_weights,
        mod_scale,
        mod_shift,
    )
    return mixed.reshape(members, rows_here, width)


def solution(mesh):
    return jax.shard_map(
        functools.partial(on_device, mesh.shape["dp"]),
        mesh=mesh,
        in_specs=(
            P("dp", "fsdp", None),
            P("fsdp", None),
            P("fsdp", None),
            P(),
            P(),
            P(),
            P(),
            P("dp", None),
            P("dp", None),
        ),
        out_specs=P("dp", "fsdp", None),
        check_vma=False,
    )
```

```python
import functools
import math

import jax
import jax.numpy as jnp
from jax import lax
from jax.experimental import pallas as pl
from jax.experimental.pallas import tpu as pltpu
from jax.sharding import PartitionSpec as P

HDIM = 128
MESH = pl.DeviceIdType.MESH
LAG = 3
KGROUPS = 4
RELAY_LAG = (2, 2, 2, 1)
ROUNDS = (
    (-1, -1, -1, -1, 10, 8, 11, 9, -1, -1, -1, 3),
    (-1, -1, -1, -1, 3, 0, 3, 11, -1, -1, -1, 2),
    (-1, -1, -1, -1, 1, 4, 1, 7, -1, -1, -1, 11),
    (19, 40, 43, 41, 42, 40, 43, 41, 19, -1, -1, 41),
    (35, 32, 35, 43, 19, 6, 35, 14, 18, -1, 35, 43),
    (33, 36, 33, 39, 6, 3, 6, 39, 42, 36, 33, 9),
    (27, 72, 40, 73, 16, 11, 40, 6, 57, 19, 75, 42),
    (59, 19, 67, 46, 5, 33, 67, 0, 51, 18, 67, 1),
    (25, 38, 38, 71, 34, 38, 75, 40, 34, 42, 34, 39),
    (74, 73, 72, 36, 11, 43, 19, 38, 58, 57, 19, 38),
    (38, 65, 99, 67, 37, 65, 18, 47, 48, 65, 99, 67),
    (55, 70, 107, 68, 18, 51, 39, 74, 17, 70, 107, 68),
    (48, 58, 51, 19, 48, 73, 51, 34, 55, 58, 51, 37),
    (39, 97, 96, 99, 39, 35, 73, 70, 69, 66, 65, 99),
    (75, 83, 19, 79, 84, 83, 5, 71, 56, 17, 18, 69),
    (80, 105, 71, 16, 80, 18, 58, 51, 53, 59, 48, 66),
    (71, 98, 105, 96, 38, 69, 66, 66, 49, 55, 105, 102),
    (116, 71, 73, 76, 33, 80, 37, 12, 116, 80, 58, 103),
    (112, 106, 90, 48, 82, 53, 17, 83, 82, 115, 50, 83),
    (72, 99, 55, 83, 118, 49, 55, 79, 118, 53, 55, 15),
    (85, 116, 80, 77, 119, 68, 80, 58, 119, 116, 104, 44),
    (67, 67, 91, 115, 117, 116, 91, 49, 114, 82, 57, 115),
    (43, 107, 87, 55, 73, 81, 87, 50, 22, 118, 53, 73),
    (60, 101, 116, 103, 31, 117, 81, 55, 23, 100, 116, 104),
    (99, 53, 88, 112, 74, 20, 123, 90, 60, 20, 88, 107),
    (40, 85, 53, 53, 89, 55, 82, 82, 26, 22, 119, 78),
    (23, 102, 100, 116, 75, 58, 119, 116, 63, 21, 118, 116),
    (96, 60, 59, 100, 15, 52, 89, 88, 24, 60, 27, 106),
    (94, 26, 27, 88, 94, 15, 53, 119, 121, 86, 22, 114),
    (107, 90, 123, 20, 58, 14, 15, 122, 94, 63, 59, 119),
    (86, 24, 60, 120, 47, 63, 121, 52, 122, 26, 56, 118),
    (126, 61, 101, 27, 126, 47, 60, 54, 126, 103, 85, 117),
    (95, 91, 47, 122, 13, 46, 47, 59, 120, 94, 60, 46),
    (79, 122, 61, 111, 56, 95, 13, 121, 89, 122, 61, 75),
    (127, 95, 92, 44, 14, 79, 92, 78, 31, 126, 92, 13),
    (92, 79, 94, -1, 45, 12, 79, 77, 30, 78, 63, 12),
    (47, 127, 45, 61, 79, 61, 45, 61, 45, 127, 94, -1),
    (124, 111, 124, -1, 76, 78, 126, 92, 29, 31, 126, -1),
    (77, 76, 111, -1, 77, -1, 78, -1, 28, 76, 95, -1),
    (-1, 124, -1, -1, -1, -1, 77, 93, -1, -1, 127, -1),
    (-1, 108, 31, -1, -1, -1, -1, 124, -1, 29, 30, 126),
    (-1, -1, -1, -1, -1, -1, -1, -1, -1, -1, 31, -1),
    (-1, -1, -1, -1, -1, -1, -1, 125, -1, -1, -1, -1),
)
ROUND_US = 1.9
QUERY_US, ATTEND_US, OUT_US = 0.27, 0.72, 0.72
LAST_SHARDS = 3


def moved(link, place, piece):
    dy, h, k, r = piece
    if link == 0:
        return place, (dy, h, k, (r + 1) % 4)
    if link == 1:
        return place, ((dy + 1) % 4, h, k, r)
    if place < 3:
        return place + 1, piece
    return 0, (dy, 1 - h, k, r)


def named(number):
    return None if number < 0 else (number // 32, number // 16 % 2, number // 4 % 4, number % 4)


def make_rounds():
    rounds = [[[named(row[link * 4 + p]) for p in range(4)] for link in range(3)] for row in ROUNDS]
    ready = [{named(n): 0 for n in range(16)} for _ in range(4)]
    for now, row in enumerate(rounds):
        for link in range(3):
            for place in range(4):
                piece = row[link][place]
                if piece is not None:
                    to, there = moved(link, place, piece)
                    assert ready[place][piece] <= now and there not in ready[to]
                    ready[to][there] = now + LAG
    assert all(len(r) == 128 for r in ready)
    return rounds, ready


def arrivals_of(rounds):
    result = []
    for row in rounds:
        got = [[None] * 4 for _ in range(3)]
        for link in range(3):
            for place in range(4):
                if row[link][place] is not None:
                    to, there = moved(link, place, row[link][place])
                    got[link][to] = there
        result.append(got)
    return result


def group_rounds(ready):
    mine, both = {}, {}
    for dy in range(4):
        for h in range(2):
            for k in range(KGROUPS):
                mine[dy, h, k] = max(ready[place][dy, h, k, r] for place in range(4) for r in range(4))
    for dy, h, k in mine:
        both[dy, h, k] = max(mine[dy, h, k], mine[(4 - dy) % 4, h, k] + RELAY_LAG[k])
        if (dy, h) == (0, 0):
            both[dy, h, k] = 0
    return mine, both


def kernel(
    n_dp,
    lat_ref,
    wq_ref,
    wo_ref,
    text_ref,
    counts_ref,
    conds_ref,
    guide_ref,
    scale_ref,
    shift_ref,
    out_ref,
    wq,
    wo,
    x_buf,
    text,
    q_acc,
    att,
    acc,
    pivot,
    distance,
    square,
    out_buf,
    send_sem,
    recv_sem,
    sib_sem,
    local_sem,
):
    rounds, ready = make_rounds()
    arrivals = arrivals_of(rounds)
    n_rounds = len(rounds)
    dp, fs = lax.axis_index("dp"), lax.axis_index("fsdp")
    core, x_at, z_lo = dp % 2, (dp // 2) % 4, dp // 8
    y_at, z_hi = fs // 2, fs % 2
    sign = 1 - 2 * core
    column = (4 + sign * x_at) % 4
    place = z_lo + core * (3 - 2 * z_lo)
    z_next = (z_hi * 4 + z_lo + 8 + sign) % 8
    z_prev = (z_hi * 4 + z_lo + 8 - sign) % 8
    targets = (
        (z_lo * 8 + ((x_at + 4 + sign) % 4) * 2 + core, fs),
        (dp, ((y_at + 4 + sign) % 4) * 2 + z_hi),
        ((z_next % 4) * 8 + x_at * 2 + core, y_at * 2 + z_next // 4),
    )
    sources = (
        (z_lo * 8 + ((x_at + 4 - sign) % 4) * 2 + core, fs),
        (dp, ((y_at + 4 - sign) % 4) * 2 + z_hi),
        ((z_prev % 4) * 8 + x_at * 2 + core, y_at * 2 + z_prev // 4),
    )
    sibling = (dp + sign, fs)

    fetches = [
        pltpu.make_async_copy(wq_ref, wq.at[fs], local_sem.at[0]),
        pltpu.make_async_copy(wo_ref, wo.at[fs], local_sem.at[1]),
        pltpu.make_async_copy(lat_ref, x_buf, local_sem.at[2]),
        pltpu.make_async_copy(text_ref, text, local_sem.at[3]),
    ]
    for fetch in fetches[:3]:
        fetch.start()
    barrier = pltpu.get_barrier_semaphore()
    for other in sources + (sibling,):
        pl.semaphore_signal(barrier, inc=1, device_id=other, device_id_type=MESH)
    pl.semaphore_wait(barrier, 4)
    fetches[0].wait()
    out_fetched = False

    shards = {
        (dy, h): ((y_at + 4 - sign * dy) % 4) * 2 + (z_hi + h) % 2 for dy in range(4) for h in range(2)
    }
    columns = [(column + 4 - r) % 4 for r in range(4)]
    row_at = (
        [core * 256 + c * 64 for c in columns],
        [core * 128 + c * 32 for c in columns],
    )

    def pick(options, of):
        keyed = {}
        for p, piece in options.items():
            key, value = of(piece)
            keyed.setdefault(key, (value, []))[1].append(p)
        groups = list(keyed.values())
        result = groups[-1][0]
        for value, places in groups[:-1]:
            here = functools.reduce(jnp.logical_or, [place == p for p in places])
            result = jnp.where(here, value, result)
        return result

    def slot(options, weight):
        shard = pick(options, lambda p: (p[:2], shards[p[:2]]))
        row = pick(options, lambda p: (p[3], row_at[weight][p[3]]))
        half = pick(options, lambda p: (p[2] % 2, p[2] % 2))
        if weight == 0:
            return wq.at[
                shard,
                pl.ds(pl.multiple_of(row, 64), 64),
                pl.ds(pl.multiple_of(half * 1024, 1024), 1024),
            ]
        return wo.at[
            shard,
            pl.ds(pl.multiple_of(row, 32), 32),
            pl.ds(pl.multiple_of(half * 2048, 2048), 2048),
        ]

    def for_places(row, action):
        for weight in range(2):
            options = {
                p: row[p] for p in range(4) if row[p] is not None and row[p][2] // 2 == weight
            }
            if not options:
                continue
            if len(options) == 4:
                action(options, weight)
            else:
                here = functools.reduce(jnp.logical_or, [place == p for p in options])
                pl.when(here)(functools.partial(action, options, weight))

    def link_copy(link, step, options, weight):
        ref = slot(options, weight)
        return pltpu.make_async_remote_copy(
            src_ref=ref,
            dst_ref=ref,
            send_sem=send_sem.at[link],
            recv_sem=recv_sem.at[link * n_rounds + step],
            device_id=targets[link],
            device_id_type=MESH,
        )

    def half_group(dy, h, k, of_core):
        shard = shards[dy, h]
        if k < 2:
            rows = pl.ds(pl.multiple_of(of_core * 256, 256), 256)
            return wq.at[shard, rows, pl.ds(k * 1024, 1024)], sib_sem.at[k * 8 + shard]
        rows = pl.ds(pl.multiple_of(of_core * 128, 128), 128)
        return wo.at[shard, rows, pl.ds((k - 2) * 2048, 2048)], sib_sem.at[k * 8 + shard]

    def relay_piece(options, weight):
        ref = slot(options, weight)
        shard = pick(options, lambda p: (p[:2], shards[p[:2]]))
        pltpu.make_async_remote_copy(
            src_ref=ref,
            dst_ref=ref,
            send_sem=send_sem.at[3],
            recv_sem=sib_sem.at[3 * 8 + shard],
            device_id=sibling,
            device_id_type=MESH,
        ).start()

    def relay(dy, h, k):
        ref, sem = half_group(dy, h, k, core)
        pltpu.make_async_remote_copy(
            src_ref=ref,
            dst_ref=ref,
            send_sem=send_sem.at[3],
            recv_sem=sem,
            device_id=sibling,
            device_id_type=MESH,
        ).start()

    def wait_sibling(dy, h, k):
        if (dy, h) != (0, 0):
            ref, sem = half_group(dy, h, k, 1 - core)
            pltpu.make_async_copy(ref, ref, sem).wait()

    def wait_sent(sem, ref):
        pltpu.make_async_copy(ref, ref, sem).wait()

    mine, both = group_rounds(ready)
    order = sorted(shards, key=lambda s: (both[s + (3,)], s))
    places_of = []
    for shard in range(8):
        back = (sign * (y_at - shard // 2) + 4) % 4
        key = back * 2 + (z_hi + shard) % 2
        at = jnp.int32(0)
        for i, (dy, h) in enumerate(order):
            at = jnp.where(key == dy * 2 + h, i, at)
        places_of.append(at * 256)

    def query_task(first, dy, h, k):
        wait_sibling(dy, h, k)
        shard = shards[dy, h]
        at = pl.ds(k * 1024, 1024)
        part = jnp.dot(
            x_buf[:, pl.ds(pl.multiple_of(shard * 512, 512), 512)],
            wq[shard, :, at],
            preferred_element_type=jnp.float32,
        )
        if first:
            q_acc[:, at] = part
        else:
            q_acc[:, at] += part

    def attend_task(shard):
        scored = []
        for p in range(2):
            head = shard * 2 + p
            queries = q_acc[:, head * HDIM : (head + 1) * HDIM].astype(jnp.bfloat16)
            for cond in range(4):
                scores = lax.dot_general(
                    queries,
                    text[cond, :, head * HDIM : (head + 1) * HDIM],
                    (((1,), (1,)), ((), ())),
                    preferred_element_type=jnp.float32,
                )
                scored.append((p, cond, scores))
        weighed = []
        for p, cond, scores in scored:
            peak = jnp.max(scores, axis=-1, keepdims=True)
            expd = jnp.exp2((scores - peak) * (math.log2(math.e) / math.sqrt(HDIM)))
            probs = (expd * (1.0 / jnp.sum(expd, axis=-1, keepdims=True))).astype(jnp.bfloat16)
            weighed.append((p, cond, probs))
        for p, cond, probs in weighed:
            value_at = 2048 + (shard * 2 + p) * HDIM
            result = jnp.dot(
                probs, text[cond, :, value_at : value_at + HDIM], preferred_element_type=jnp.float32
            )
            at = pl.ds(pl.multiple_of(places_of[shard] + p * HDIM, HDIM), HDIM)
            att[pl.ds(cond * 128, 128), at] = result.astype(jnp.bfloat16)

    def tally(rows, value, width, first):
        if first:
            center = jnp.sum(value, axis=-1, keepdims=True) / width
            from_here = jnp.broadcast_to(center, (128, 128))
            pivot[rows] = from_here
            summed = jnp.zeros((128, 128), jnp.float32)
            squared = jnp.zeros((128, 128), jnp.float32)
        else:
            from_here, summed, squared = pivot[rows], distance[rows], square[rows]
        for j in range(0, width, 128):
            moved_h = value[:, j : j + 128] - from_here
            summed += moved_h
            squared += moved_h * moved_h
        distance[rows] = summed
        square[rows] = squared

    def out_task(low, high, start, width, k):
        if start == (k - 2) * 2048:
            for dy, h in order[low:high]:
                wait_sibling(dy, h, k)
        at = pl.ds(start, width)
        part = jnp.dot(
            att[:, low * 256 : high * 256],
            jnp.concatenate([wo[shards[s], :, at] for s in order[low:high]], axis=0),
            preferred_element_type=jnp.float32,
        )
        base = x_buf[:, at].astype(jnp.float32)
        for c in range(4):
            rows = slice(c * 128, c * 128 + 128)
            if low == 0:
                value = part[rows] + base
            else:
                value = part[rows] + acc[rows, at]
            acc[rows, at] = value
            if k == 2 or low > 0:
                tally(rows, value, width, k == 2 and start == 0)

    tasks = []
    for k in range(2):
        stage = 2 * k
        for i, s in enumerate(sorted(shards, key=lambda s: (both[s + (k,)], s))):
            call = functools.partial(query_task, i == 0, *s, k)
            tasks.append((stage, -1, both[s + (k,)], QUERY_US, call))
        for shard in range(4 * k, 4 * k + 4):
            call = functools.partial(attend_task, shard)
            tasks.append((stage + 1, stage, 0, ATTEND_US, call))
    cut = 8 - LAST_SHARDS
    when = max(both[s + (2,)] for s in order)
    for start in range(0, 2048, 256):
        call = functools.partial(out_task, 0, 8, start, 256, 2)
        tasks.append((4, 3, when, OUT_US, call))
    for low, high, stage in ((0, cut, 6), (cut, 8, 7)):
        when = max(both[s + (3,)] for s in order[low:high])
        for start in range(2048, 4096, 512):
            call = functools.partial(out_task, low, high, start, 512, 3)
            after = 4 if stage == 6 else 6
            tasks.append((stage, after, when, OUT_US * 2 * (high - low) / 8, call))

    def next_task(step, budget):
        for i, (stage, after, when, cost, call) in enumerate(tasks):
            if when <= step and cost <= budget and not any(t[0] <= after for t in tasks):
                tasks.pop(i)
                return cost, call
        return None

    fetched = False
    for step in range(n_rounds + LAG):
        came = step - LAG
        if came >= 0:
            for link in range(3):
                for_places(
                    arrivals[came][link],
                    lambda options, weight, link=link: link_copy(
                        link, came, options, weight
                    ).wait_recv(),
                )
        if step < n_rounds:
            if not out_fetched and any(p is not None and p[2] > 1 for got in rounds[step] for p in got):
                fetches[1].wait()
                out_fetched = True
            for link in range(3):
                for_places(
                    rounds[step][link],
                    lambda options, weight, link=link: link_copy(
                        link, step, options, weight
                    ).start(),
                )
            if step == 0:
                fetches[3].start()
        if came >= 0:
            for link in range(3):
                last_group = [p if p is not None and p[2] == 3 else None for p in arrivals[came][link]]
                for_places(last_group, relay_piece)
        for group in mine:
            if mine[group] == step and step > 0 and group[2] < 3:
                relay(*group)
        if step >= 1:
            if not fetched:
                fetches[2].wait()
                fetches[3].wait()
                fetched = True
            budget = ROUND_US
            while (found := next_task(step, budget)) is not None:
                budget -= found[0]
                found[1]()
    while tasks:
        next_task(1 << 20, 1 << 20)[1]()

    @pl.loop(0, 4)
    def _(member):
        latent = dp * 4 + member
        count = counts_ref[latent]
        total = jnp.int32(0)
        weights = [jnp.int32(0)] * 4
        for s in range(4):
            weight = jnp.where(s < count, guide_ref[s], 0)
            total = total + weight
            cond = conds_ref[s, latent]
            weights = [w + jnp.where(cond == c, weight, 0) for c, w in enumerate(weights)]
        share = 1.0 / jnp.full((32, 1), total.astype(jnp.float32))
        scale = 1.0 + scale_ref[pl.ds(member, 1), :]
        shift = shift_ref[pl.ds(member, 1), :]
        start = pl.multiple_of(member * 32, 32)
        rows = [pl.ds(pl.multiple_of(c * 128 + start, 32), 32) for c in range(4)]
        spans = [slice(j, j + 128) for j in range(0, 4096, 128)]
        gains, offset = [], jnp.zeros((32, 1), jnp.float32)
        for c in range(4):
            shift_c = jnp.sum(distance[rows[c]], axis=-1, keepdims=True) / 4096
            spread = jnp.sum(square[rows[c]], axis=-1, keepdims=True) / 4096 - shift_c * shift_c
            spread = jnp.maximum(spread, 0.0)
            gain = lax.rsqrt(spread + 1e-06) * (weights[c].astype(jnp.float32) * share)
            gains.append(gain)
            offset += (pivot[rows[c], :1] + shift_c) * gain
        for at in spans:
            numer = -offset
            for c in range(4):
                numer += acc[rows[c], at] * gains[c]
            combined = numer.astype(jnp.bfloat16).astype(jnp.float32)
            out_buf[pl.ds(start, 32), at] = (
                combined * scale[:, at] + shift[:, at]
            ).astype(jnp.bfloat16)
        done = pl.ds(start, 32)
        pltpu.make_async_copy(out_buf.at[done], out_ref.at[done], local_sem.at[4]).start()

    for link in range(3):
        sends = [sum(row[link][p] is not None for row in rounds) for p in range(4)]
        for many in sorted(set(sends)):
            here = functools.reduce(
                jnp.logical_or, [place == p for p in range(4) if sends[p] == many]
            )
            pl.when(here)(
                functools.partial(wait_sent, send_sem.at[link], acc.at[pl.ds(0, many * 8)])
            )
    wait_sent(send_sem.at[3], wq.at[pl.ds(0, 7)])
    pltpu.make_async_copy(out_buf, out_ref, local_sem.at[4]).wait()


def on_device(
    n_dp,
    latents,
    w_query,
    w_out,
    text_cache,
    branch_counts,
    branch_conds,
    guide_weights,
    mod_scale,
    mod_shift,
):
    members, rows_here, width = latents.shape
    rows = members * rows_here
    n_rounds = len(make_rounds()[0])
    anywhere = pl.BlockSpec(memory_space=pl.ANY)
    in_vmem = pl.BlockSpec(memory_space=pltpu.VMEM)
    in_smem = pl.BlockSpec(memory_space=pltpu.SMEM)
    mixed = pl.pallas_call(
        functools.partial(kernel, n_dp),
        out_shape=jax.ShapeDtypeStruct((rows, width), jnp.bfloat16),
        in_specs=[anywhere] * 4 + [in_smem] * 3 + [in_vmem] * 2,
        out_specs=anywhere,
        scratch_shapes=[
            pltpu.VMEM((8, 512, 2048), jnp.bfloat16),
            pltpu.VMEM((8, 256, 4096), jnp.bfloat16),
            pltpu.VMEM((rows, width), jnp.bfloat16),
            pltpu.VMEM(text_cache.shape, jnp.bfloat16),
            pltpu.VMEM((rows, 2048), jnp.float32),
            pltpu.VMEM((4 * rows, 2048), jnp.bfloat16),
            pltpu.VMEM((4 * rows, width), jnp.float32),
            pltpu.VMEM((4 * rows, 128), jnp.float32),
            pltpu.VMEM((4 * rows, 128), jnp.float32),
            pltpu.VMEM((4 * rows, 128), jnp.float32),
            pltpu.VMEM((rows, width), jnp.bfloat16),
            pltpu.SemaphoreType.DMA((4,)),
            pltpu.SemaphoreType.DMA((3 * n_rounds,)),
            pltpu.SemaphoreType.DMA((8 * KGROUPS,)),
            pltpu.SemaphoreType.DMA((5,)),
        ],
        compiler_params=pltpu.CompilerParams(
            collective_id=0, has_side_effects=True, vmem_limit_bytes=58 * 2**20
        ),
        name="gather_and_attend",
    )(
        latents.reshape(rows, width),
        w_query,
        w_out,
        text_cache,
        branch_counts,
        branch_conds.T,
        guide_weights,
        mod_scale,
        mod_shift,
    )
    return mixed.reshape(members, rows_here, width)


def solution(mesh):
    return jax.shard_map(
        functools.partial(on_device, mesh.shape["dp"]),
        mesh=mesh,
        in_specs=(
            P("dp", "fsdp", None),
            P("fsdp", None),
            P("fsdp", None),
            P(),
            P(),
            P(),
            P(),
            P("dp", None),
            P("dp", None),
        ),
        out_specs=P("dp", "fsdp", None),
        check_vma=False,
    )
```

```python
import functools
import math

import jax
import jax.numpy as jnp
from jax import lax
from jax.experimental import pallas as pl
from jax.experimental.pallas import tpu as pltpu
from jax.sharding import PartitionSpec as P

HDIM = 128
MESH = pl.DeviceIdType.MESH
LAG = 3
KGROUPS = 4
RELAY_LAG = (2, 2, 2, 1)
ROUNDS = (
    (-1, -1, -1, -1, 4, 4, 3, 7, -1, -1, -1, 5),
    (-1, -1, -1, -1, 6, 5, 2, 3, -1, -1, -1, 7),
    (-1, -1, -1, -1, 7, 6, 7, 6, -1, -1, -1, 0),
    (21, -1, 35, 39, 36, 7, 35, 39, 21, 36, -1, 39),
    (23, -1, -1, 35, 38, 37, 8, 35, 23, 37, 34, 9),
    (16, -1, -1, -1, 39, 38, 39, 38, 16, 38, -1, 3),
    (68, 21, 67, 36, 3, 21, 67, 36, 68, 21, -1, 36),
    (36, 23, 40, 32, 21, 39, 37, 67, 25, 23, 40, 67),
    (17, 16, 71, 67, 71, 70, 71, 34, 19, 70, -1, 34),
    (35, 53, 21, 68, 25, 68, 64, 68, 52, 16, 21, 32),
    (53, 25, 23, 40, 53, 71, 69, 40, 83, 53, 23, 99),
    (103, 17, 103, 64, 19, 53, 23, 66, 50, 102, 103, 66),
    (32, 100, 16, 21, 69, 54, 41, 69, 48, 54, 96, 12),
    (85, 54, 96, 23, 85, 1, 53, 72, 115, 83, 53, 72),
    (115, 50, 55, 72, 82, 3, 55, 65, 82, 26, 16, 103),
    (101, 48, 17, 101, 9, 48, 17, 22, 28, 50, 17, 65),
    (28, 115, 83, 104, 88, 55, 83, 53, 117, 33, 83, 64),
    (112, 33, 73, 73, 8, 35, 26, 16, 114, 82, 26, 73),
    (117, 28, 18, 17, 41, 86, 49, 54, 81, 51, 49, 40),
    (86, 112, 85, 83, 120, 87, 52, 83, 32, 117, 50, 33),
    (119, 67, 115, 26, 52, 67, 58, 23, 120, 28, 82, 74),
    (29, 29, 97, 18, 2, 26, 81, 74, 56, 48, 81, 105),
    (73, 87, 117, 115, 14, 34, 82, 11, 24, 29, 51, 115),
    (90, 99, 90, 27, 33, 33, 74, 82, 116, 120, 28, 80),
    (30, 30, 58, 55, 34, 58, 33, 81, 121, 56, 90, 106),
    (99, 56, 29, 86, 46, 56, 73, 43, 73, 24, 117, 43),
    (74, 96, 120, 28, 65, 66, 84, 27, 89, 66, 120, 114),
    (66, 90, 56, 106, 74, 90, 56, 52, 40, 31, 58, 11),
    (122, 73, 24, 117, 40, 12, 91, 90, 59, 119, 91, 10),
    (57, 26, 121, 120, 75, 10, 10, 87, 78, 89, 116, 59),
    (78, 40, 106, 41, 29, 40, 31, 24, 106, -1, 88, 58),
    (46, 122, 74, 122, 28, 73, 123, 15, 75, 44, 25, 120),
    (-1, 78, 42, 29, 12, 78, 14, 13, 43, 78, 89, 121),
    (79, 106, 107, 56, 61, 72, 63, 29, 61, 72, 31, -1),
    (61, 44, 44, 47, 60, 14, 44, 47, 47, -1, 63, 47),
    (44, 110, 46, 45, 79, 44, 30, 45, 60, 110, 78, -1),
    (93, 61, 95, 61, 93, 31, 95, 61, 93, 79, 95, -1),
    (76, -1, 76, 79, 92, 45, 76, 79, 92, 61, -1, 79),
    (111, 111, 110, 63, 78, -1, 62, 77, -1, 60, 110, -1),
    (125, 93, 92, 95, -1, 63, 92, 62, 125, -1, 127, -1),
    (-1, -1, 108, 111, 77, 77, -1, 93, 124, -1, -1, 111),
    (-1, -1, -1, -1, -1, -1, 94, -1, -1, -1, -1, -1),
    (-1, 125, 124, 127, -1, 95, -1, 94, -1, -1, -1, -1),
)
ROUND_US = 1.9
QUERY_US, ATTEND_US, OUT_US = 0.27, 0.72, 0.72
LAST_SHARDS = 3


def moved(link, place, piece):
    dy, h, k, r = piece
    if link == 0:
        return place, (dy, h, k, (r + 1) % 4)
    if link == 1:
        return place, ((dy + 1) % 4, h, k, r)
    if place < 3:
        return place + 1, piece
    return 0, (dy, 1 - h, k, r)


def named(number):
    return None if number < 0 else (number // 32, number // 16 % 2, number // 4 % 4, number % 4)


def make_rounds():
    rounds = [[[named(row[link * 4 + p]) for p in range(4)] for link in range(3)] for row in ROUNDS]
    ready = [{named(n): 0 for n in range(16)} for _ in range(4)]
    for now, row in enumerate(rounds):
        for link in range(3):
            for place in range(4):
                piece = row[link][place]
                if piece is not None:
                    to, there = moved(link, place, piece)
                    assert ready[place][piece] <= now and there not in ready[to]
                    ready[to][there] = now + LAG
    assert all(len(r) == 128 for r in ready)
    return rounds, ready


def arrivals_of(rounds):
    result = []
    for row in rounds:
        got = [[None] * 4 for _ in range(3)]
        for link in range(3):
            for place in range(4):
                if row[link][place] is not None:
                    to, there = moved(link, place, row[link][place])
                    got[link][to] = there
        result.append(got)
    return result


def group_rounds(ready):
    mine, both = {}, {}
    for dy in range(4):
        for h in range(2):
            for k in range(KGROUPS):
                mine[dy, h, k] = max(ready[place][dy, h, k, r] for place in range(4) for r in range(4))
    for dy, h, k in mine:
        both[dy, h, k] = max(mine[dy, h, k], mine[(4 - dy) % 4, h, k] + RELAY_LAG[k])
        if (dy, h) == (0, 0):
            both[dy, h, k] = 0
    return mine, both


def kernel(
    n_dp,
    lat_ref,
    wq_ref,
    wo_ref,
    text_ref,
    counts_ref,
    conds_ref,
    guide_ref,
    scale_ref,
    shift_ref,
    out_ref,
    wq,
    wo,
    x_buf,
    text,
    q_acc,
    att,
    acc,
    pivot,
    distance,
    square,
    out_buf,
    send_sem,
    recv_sem,
    sib_sem,
    local_sem,
):
    rounds, ready = make_rounds()
    arrivals = arrivals_of(rounds)
    n_rounds = len(rounds)
    dp, fs = lax.axis_index("dp"), lax.axis_index("fsdp")
    core, x_at, z_lo = dp % 2, (dp // 2) % 4, dp // 8
    y_at, z_hi = fs // 2, fs % 2
    sign = 1 - 2 * core
    column = (4 + sign * x_at) % 4
    place = z_lo + core * (3 - 2 * z_lo)
    z_next = (z_hi * 4 + z_lo + 8 + sign) % 8
    z_prev = (z_hi * 4 + z_lo + 8 - sign) % 8
    targets = (
        (z_lo * 8 + ((x_at + 4 + sign) % 4) * 2 + core, fs),
        (dp, ((y_at + 4 + sign) % 4) * 2 + z_hi),
        ((z_next % 4) * 8 + x_at * 2 + core, y_at * 2 + z_next // 4),
    )
    sources = (
        (z_lo * 8 + ((x_at + 4 - sign) % 4) * 2 + core, fs),
        (dp, ((y_at + 4 - sign) % 4) * 2 + z_hi),
        ((z_prev % 4) * 8 + x_at * 2 + core, y_at * 2 + z_prev // 4),
    )
    sibling = (dp + sign, fs)

    fetches = [
        pltpu.make_async_copy(wq_ref, wq.at[fs], local_sem.at[0]),
        pltpu.make_async_copy(wo_ref, wo.at[fs], local_sem.at[1]),
        pltpu.make_async_copy(lat_ref, x_buf, local_sem.at[2]),
        pltpu.make_async_copy(text_ref, text, local_sem.at[3]),
    ]
    for fetch in fetches[:3]:
        fetch.start()
    barrier = pltpu.get_barrier_semaphore()
    for other in sources + (sibling,):
        pl.semaphore_signal(barrier, inc=1, device_id=other, device_id_type=MESH)
    pl.semaphore_wait(barrier, 4)
    fetches[0].wait()
    out_fetched = False

    shards = {
        (dy, h): ((y_at + 4 - sign * dy) % 4) * 2 + (z_hi + h) % 2 for dy in range(4) for h in range(2)
    }
    columns = [(column + 4 - r) % 4 for r in range(4)]
    row_at = (
        [core * 256 + c * 64 for c in columns],
        [core * 128 + c * 32 for c in columns],
    )

    def pick(options, of):
        keyed = {}
        for p, piece in options.items():
            key, value = of(piece)
            keyed.setdefault(key, (value, []))[1].append(p)
        groups = list(keyed.values())
        result = groups[-1][0]
        for value, places in groups[:-1]:
            here = functools.reduce(jnp.logical_or, [place == p for p in places])
            result = jnp.where(here, value, result)
        return result

    def slot(options, weight):
        shard = pick(options, lambda p: (p[:2], shards[p[:2]]))
        row = pick(options, lambda p: (p[3], row_at[weight][p[3]]))
        half = pick(options, lambda p: (p[2] % 2, p[2] % 2))
        if weight == 0:
            return wq.at[
                shard,
                pl.ds(pl.multiple_of(row, 64), 64),
                pl.ds(pl.multiple_of(half * 1024, 1024), 1024),
            ]
        return wo.at[
            shard,
            pl.ds(pl.multiple_of(row, 32), 32),
            pl.ds(pl.multiple_of(half * 2048, 2048), 2048),
        ]

    def for_places(row, action):
        for weight in range(2):
            options = {
                p: row[p] for p in range(4) if row[p] is not None and row[p][2] // 2 == weight
            }
            if not options:
                continue
            if len(options) == 4:
                action(options, weight)
            else:
                here = functools.reduce(jnp.logical_or, [place == p for p in options])
                pl.when(here)(functools.partial(action, options, weight))

    def link_copy(link, step, options, weight):
        ref = slot(options, weight)
        return pltpu.make_async_remote_copy(
            src_ref=ref,
            dst_ref=ref,
            send_sem=send_sem.at[link],
            recv_sem=recv_sem.at[link * n_rounds + step],
            device_id=targets[link],
            device_id_type=MESH,
        )

    def half_group(dy, h, k, of_core):
        shard = shards[dy, h]
        if k < 2:
            rows = pl.ds(pl.multiple_of(of_core * 256, 256), 256)
            return wq.at[shard, rows, pl.ds(k * 1024, 1024)], sib_sem.at[k * 8 + shard]
        rows = pl.ds(pl.multiple_of(of_core * 128, 128), 128)
        return wo.at[shard, rows, pl.ds((k - 2) * 2048, 2048)], sib_sem.at[k * 8 + shard]

    def relay_piece(options, weight):
        ref = slot(options, weight)
        shard = pick(options, lambda p: (p[:2], shards[p[:2]]))
        pltpu.make_async_remote_copy(
            src_ref=ref,
            dst_ref=ref,
            send_sem=send_sem.at[3],
            recv_sem=sib_sem.at[3 * 8 + shard],
            device_id=sibling,
            device_id_type=MESH,
        ).start()

    def relay(dy, h, k):
        ref, sem = half_group(dy, h, k, core)
        pltpu.make_async_remote_copy(
            src_ref=ref,
            dst_ref=ref,
            send_sem=send_sem.at[3],
            recv_sem=sem,
            device_id=sibling,
            device_id_type=MESH,
        ).start()

    def wait_sibling(dy, h, k):
        if (dy, h) != (0, 0):
            ref, sem = half_group(dy, h, k, 1 - core)
            pltpu.make_async_copy(ref, ref, sem).wait()

    def wait_sent(sem, ref):
        pltpu.make_async_copy(ref, ref, sem).wait()

    mine, both = group_rounds(ready)
    order = sorted(shards, key=lambda s: (both[s + (3,)], s))
    places_of = []
    for shard in range(8):
        back = (sign * (y_at - shard // 2) + 4) % 4
        key = back * 2 + (z_hi + shard) % 2
        at = jnp.int32(0)
        for i, (dy, h) in enumerate(order):
            at = jnp.where(key == dy * 2 + h, i, at)
        places_of.append(at * 256)

    def query_task(first, dy, h, k):
        wait_sibling(dy, h, k)
        shard = shards[dy, h]
        at = pl.ds(k * 1024, 1024)
        part = jnp.dot(
            x_buf[:, pl.ds(pl.multiple_of(shard * 512, 512), 512)],
            wq[shard, :, at],
            preferred_element_type=jnp.float32,
        )
        if first:
            q_acc[:, at] = part
        else:
            q_acc[:, at] += part

    def attend_task(shard):
        scored = []
        for p in range(2):
            head = shard * 2 + p
            queries = q_acc[:, head * HDIM : (head + 1) * HDIM].astype(jnp.bfloat16)
            for cond in range(4):
                scores = lax.dot_general(
                    queries,
                    text[cond, :, head * HDIM : (head + 1) * HDIM],
                    (((1,), (1,)), ((), ())),
                    preferred_element_type=jnp.float32,
                )
                scored.append((p, cond, scores))
        weighed = []
        for p, cond, scores in scored:
            peak = jnp.max(scores, axis=-1, keepdims=True)
            expd = jnp.exp2((scores - peak) * (math.log2(math.e) / math.sqrt(HDIM)))
            probs = (expd * (1.0 / jnp.sum(expd, axis=-1, keepdims=True))).astype(jnp.bfloat16)
            weighed.append((p, cond, probs))
        for p, cond, probs in weighed:
            value_at = 2048 + (shard * 2 + p) * HDIM
            result = jnp.dot(
                probs, text[cond, :, value_at : value_at + HDIM], preferred_element_type=jnp.float32
            )
            at = pl.ds(pl.multiple_of(places_of[shard] + p * HDIM, HDIM), HDIM)
            att[pl.ds(cond * 128, 128), at] = result.astype(jnp.bfloat16)

    def tally(rows, value, width, first):
        if first:
            center = jnp.sum(value, axis=-1, keepdims=True) / width
            from_here = jnp.broadcast_to(center, (128, 128))
            pivot[rows] = from_here
            summed = jnp.zeros((128, 128), jnp.float32)
            squared = jnp.zeros((128, 128), jnp.float32)
        else:
            from_here, summed, squared = pivot[rows], distance[rows], square[rows]
        for j in range(0, width, 128):
            moved_h = value[:, j : j + 128] - from_here
            summed += moved_h
            squared += moved_h * moved_h
        distance[rows] = summed
        square[rows] = squared

    def out_task(low, high, start, width, k):
        if start == (k - 2) * 2048:
            for dy, h in order[low:high]:
                wait_sibling(dy, h, k)
        at = pl.ds(start, width)
        part = jnp.dot(
            att[:, low * 256 : high * 256],
            jnp.concatenate([wo[shards[s], :, at] for s in order[low:high]], axis=0),
            preferred_element_type=jnp.float32,
        )
        base = x_buf[:, at].astype(jnp.float32)
        for c in range(4):
            rows = slice(c * 128, c * 128 + 128)
            if low == 0:
                value = part[rows] + base
            else:
                value = part[rows] + acc[rows, at]
            acc[rows, at] = value
            if k == 2 or low > 0:
                tally(rows, value, width, k == 2 and start == 0)

    tasks = []
    for k in range(2):
        stage = 2 * k
        for i, s in enumerate(sorted(shards, key=lambda s: (both[s + (k,)], s))):
            call = functools.partial(query_task, i == 0, *s, k)
            tasks.append((stage, -1, both[s + (k,)], QUERY_US, call))
        for shard in range(4 * k, 4 * k + 4):
            call = functools.partial(attend_task, shard)
            tasks.append((stage + 1, stage, 0, ATTEND_US, call))
    cut = 8 - LAST_SHARDS
    when = max(both[s + (2,)] for s in order)
    for start in range(0, 2048, 256):
        call = functools.partial(out_task, 0, 8, start, 256, 2)
        tasks.append((4, 3, when, OUT_US, call))
    for low, high, stage in ((0, cut, 6), (cut, 8, 7)):
        when = max(both[s + (3,)] for s in order[low:high])
        for start in range(2048, 4096, 512):
            call = functools.partial(out_task, low, high, start, 512, 3)
            after = 4 if stage == 6 else 6
            tasks.append((stage, after, when, OUT_US * 2 * (high - low) / 8, call))

    def next_task(step, budget):
        for i, (stage, after, when, cost, call) in enumerate(tasks):
            if when <= step and cost <= budget and not any(t[0] <= after for t in tasks):
                tasks.pop(i)
                return cost, call
        return None

    fetched = False
    for step in range(n_rounds + LAG):
        came = step - LAG
        if came >= 0:
            for link in range(3):
                for_places(
                    arrivals[came][link],
                    lambda options, weight, link=link: link_copy(
                        link, came, options, weight
                    ).wait_recv(),
                )
        if step < n_rounds:
            if not out_fetched and any(p is not None and p[2] > 1 for got in rounds[step] for p in got):
                fetches[1].wait()
                out_fetched = True
            for link in range(3):
                for_places(
                    rounds[step][link],
                    lambda options, weight, link=link: link_copy(
                        link, step, options, weight
                    ).start(),
                )
            if step == 0:
                fetches[3].start()
        if came >= 0:
            for link in range(3):
                last_group = [p if p is not None and p[2] == 3 else None for p in arrivals[came][link]]
                for_places(last_group, relay_piece)
        for group in mine:
            if mine[group] == step and step > 0 and group[2] < 3:
                relay(*group)
        if step >= 1:
            if not fetched:
                fetches[2].wait()
                fetches[3].wait()
                fetched = True
            budget = ROUND_US
            while (found := next_task(step, budget)) is not None:
                budget -= found[0]
                found[1]()
    while tasks:
        next_task(1 << 20, 1 << 20)[1]()

    @pl.loop(0, 4)
    def _(member):
        latent = dp * 4 + member
        count = counts_ref[latent]
        total = jnp.int32(0)
        weights = [jnp.int32(0)] * 4
        for s in range(4):
            weight = jnp.where(s < count, guide_ref[s], 0)
            total = total + weight
            cond = conds_ref[s, latent]
            weights = [w + jnp.where(cond == c, weight, 0) for c, w in enumerate(weights)]
        share = 1.0 / jnp.full((32, 1), total.astype(jnp.float32))
        scale = 1.0 + scale_ref[pl.ds(member, 1), :]
        shift = shift_ref[pl.ds(member, 1), :]
        start = pl.multiple_of(member * 32, 32)
        rows = [pl.ds(pl.multiple_of(c * 128 + start, 32), 32) for c in range(4)]
        spans = [slice(j, j + 128) for j in range(0, 4096, 128)]
        gains, offset = [], jnp.zeros((32, 1), jnp.float32)
        for c in range(4):
            shift_c = jnp.sum(distance[rows[c]], axis=-1, keepdims=True) / 4096
            spread = jnp.sum(square[rows[c]], axis=-1, keepdims=True) / 4096 - shift_c * shift_c
            spread = jnp.maximum(spread, 0.0)
            gain = lax.rsqrt(spread + 1e-06) * (weights[c].astype(jnp.float32) * share)
            gains.append(gain)
            offset += (pivot[rows[c], :1] + shift_c) * gain
        for at in spans:
            numer = -offset
            for c in range(4):
                numer += acc[rows[c], at] * gains[c]
            combined = numer.astype(jnp.bfloat16).astype(jnp.float32)
            out_buf[pl.ds(start, 32), at] = (
                combined * scale[:, at] + shift[:, at]
            ).astype(jnp.bfloat16)
        done = pl.ds(start, 32)
        pltpu.make_async_copy(out_buf.at[done], out_ref.at[done], local_sem.at[4]).start()

    for link in range(3):
        sends = [sum(row[link][p] is not None for row in rounds) for p in range(4)]
        for many in sorted(set(sends)):
            here = functools.reduce(
                jnp.logical_or, [place == p for p in range(4) if sends[p] == many]
            )
            pl.when(here)(
                functools.partial(wait_sent, send_sem.at[link], acc.at[pl.ds(0, many * 8)])
            )
    wait_sent(send_sem.at[3], wq.at[pl.ds(0, 7)])
    pltpu.make_async_copy(out_buf, out_ref, local_sem.at[4]).wait()


def on_device(
    n_dp,
    latents,
    w_query,
    w_out,
    text_cache,
    branch_counts,
    branch_conds,
    guide_weights,
    mod_scale,
    mod_shift,
):
    members, rows_here, width = latents.shape
    rows = members * rows_here
    n_rounds = len(make_rounds()[0])
    anywhere = pl.BlockSpec(memory_space=pl.ANY)
    in_vmem = pl.BlockSpec(memory_space=pltpu.VMEM)
    in_smem = pl.BlockSpec(memory_space=pltpu.SMEM)
    mixed = pl.pallas_call(
        functools.partial(kernel, n_dp),
        out_shape=jax.ShapeDtypeStruct((rows, width), jnp.bfloat16),
        in_specs=[anywhere] * 4 + [in_smem] * 3 + [in_vmem] * 2,
        out_specs=anywhere,
        scratch_shapes=[
            pltpu.VMEM((8, 512, 2048), jnp.bfloat16),
            pltpu.VMEM((8, 256, 4096), jnp.bfloat16),
            pltpu.VMEM((rows, width), jnp.bfloat16),
            pltpu.VMEM(text_cache.shape, jnp.bfloat16),
            pltpu.VMEM((rows, 2048), jnp.float32),
            pltpu.VMEM((4 * rows, 2048), jnp.bfloat16),
            pltpu.VMEM((4 * rows, width), jnp.float32),
            pltpu.VMEM((4 * rows, 128), jnp.float32),
            pltpu.VMEM((4 * rows, 128), jnp.float32),
            pltpu.VMEM((4 * rows, 128), jnp.float32),
            pltpu.VMEM((rows, width), jnp.bfloat16),
            pltpu.SemaphoreType.DMA((4,)),
            pltpu.SemaphoreType.DMA((3 * n_rounds,)),
            pltpu.SemaphoreType.DMA((8 * KGROUPS,)),
            pltpu.SemaphoreType.DMA((5,)),
        ],
        compiler_params=pltpu.CompilerParams(
            collective_id=0, has_side_effects=True, vmem_limit_bytes=58 * 2**20
        ),
        name="gather_and_attend",
    )(
        latents.reshape(rows, width),
        w_query,
        w_out,
        text_cache,
        branch_counts,
        branch_conds.T,
        guide_weights,
        mod_scale,
        mod_shift,
    )
    return mixed.reshape(members, rows_here, width)


def solution(mesh):
    return jax.shard_map(
        functools.partial(on_device, mesh.shape["dp"]),
        mesh=mesh,
        in_specs=(
            P("dp", "fsdp", None),
            P("fsdp", None),
            P("fsdp", None),
            P(),
            P(),
            P(),
            P(),
            P("dp", None),
            P("dp", None),
        ),
        out_specs=P("dp", "fsdp", None),
        check_vma=False,
    )
```
